256 devices in a mesh: field: 16 (over z_hi, y), space: 16 (over z_lo, x, core).
Axes of the slice: x: 4, y: 4, z: 8 (z_hi: 4, z_lo: 2; z = z_hi * 2 + z_lo), core: 2. Of those that a mesh axis runs over, the one named last changes fastest.
Arguments:
- fields: float32 [3, 64, 1024, 1024], P(None, 'field', 'space'), may hold values from -6 to 6
- increments: float32 [3, 64, 1024, 1024], P(None, 'field', 'space'), may hold values from -6 to 6
- velocity: float32 [2, 1024, 1024], P(None, 'space', 'field'), may hold values from -25 to 25
- geometry: int32 [1024, 1024], P('space'), may hold values from 0 to 1, as said below
Outputs:
- fields_new: float32 [3, 64, 1024, 1024], P(None, 'field', 'space')
- velocity_new: float32 [2, 1024, 1024], P(None, 'space', 'field')
The draws below stay inside these ranges and needn't reach their ends.
Inputs may be any that keep to these rules, and one draw needn't show every extreme that they name: `geometry`: the walls occupy a band of rows at each side of the grid, the same width on both, over all columns from some column to the last.
All inputs are finite; a program needn't handle non-finite values. Where the reference program divides by a largest or mean magnitude, that divisor is 1e-20 or more.
Results may differ from the reference program's by a relative error of at most 0.0003.
Values sent between devices are 32-bit elements; how exact they have to be, the bound alone decides.
A program may use at most 64 MiB of HBM per device.

```python
import math
import jax
import jax.numpy as jnp
from jax import lax

ITERS = 8
FIELDS = 64
NX = 1024
NY = 1024


def draw_velocity(key, part):
    first, second, third = jax.random.split(jax.random.fold_in(key, 11), 3)
    row_scale = jnp.exp(jax.random.uniform(second, (1, NX, 1), jnp.float32, math.log(0.5), math.log(2.5)))
    col_scale = jnp.exp(jax.random.uniform(third, (1, 1, NY), jnp.float32, math.log(0.5), math.log(2.5)))
    base = jnp.clip(jax.random.normal(first, (2, NX, NY), jnp.float32), -4.0, 4.0)
    return (base * row_scale * col_scale).astype(jnp.float32)


def draw_geometry(key, part):
    first, second = jax.random.split(jax.random.fold_in(key, 23), 2)
    band = jax.random.randint(first, (), NX // 8, 3 * NX // 8 + 1)
    opening = jax.random.randint(second, (), NY // 4, 3 * NY // 4)
    row_index = lax.broadcasted_iota(jnp.int32, (NX, NY), 0)
    col_index = lax.broadcasted_iota(jnp.int32, (NX, NY), 1)
    walled = ((row_index < band) | (row_index >= NX - band)) & (col_index >= opening)
    return jnp.where(walled, 0, 1).astype(jnp.int32)


def raised(entries, rng, source, target, blocks, factor):
    def block_of(axis_at):
        return (jnp.arange(entries.shape[axis_at]) // (entries.shape[axis_at] // blocks)).reshape((-1,) + (1,) * (entries.ndim - 1 - axis_at))

    one_side = jax.random.permutation(rng, blocks)[block_of(target)]
    second = (block_of(target) + blocks // 2) % blocks
    return jnp.where((block_of(source) == one_side) | (block_of(source) == second), factor * entries, entries)


def shard_levels(key, dims, shards, smallest, high):
    def one(axis_at, shards_of):
        heights = jax.random.uniform(jax.random.fold_in(jax.random.fold_in(key, 6), axis_at), (shards_of,), jnp.float32, smallest / len(shards), high / len(shards))
        return jnp.repeat(jnp.exp(heights), dims[axis_at] // shards_of).reshape((-1,) + (1,) * (len(dims) - axis_at - 1))

    level = one(*shards[0])
    for cut in shards[1:]:
        level = level * one(*cut)
    return level


def bell_draw(own_key, extent, width, most, cuts=(), kind=jnp.bfloat16):
    drawn = jax.random.normal(own_key, extent, jnp.float32) * width
    if len(cuts) > 0:
        drawn = shard_levels(own_key, extent, cuts, -0.22, 0.18) * drawn
    return jnp.clip(drawn, min=-most, max=most).astype(kind)


def noise_with(stream_key, shape, width, bound, cuts, heavy, kind=jnp.bfloat16):
    values = width * jax.random.normal(stream_key, shape, jnp.float32)
    if cuts:
        values = values * shard_levels(stream_key, shape, cuts, -0.22, 0.18)
    return jnp.clip(raised(values, jax.random.fold_in(stream_key, 3), *heavy), -bound, bound).astype(kind)


def setup_inputs(seed: int = 0) -> dict:
    keys = jax.random.split(jax.random.key(seed), 5)
    return {
        "fields": noise_with(keys[0], (3, FIELDS, NX, NY), 1.0, 6.0, ((1, 16), (2, 16)), (1, 3, 16, 2.0), jnp.float32),
        "increments": bell_draw(keys[1], (3, FIELDS, NX, NY), 1.0, 6.0, ((1, 16), (2, 16)), jnp.float32),
        "velocity": draw_velocity(jax.random.fold_in(keys[4], 71), 0),
        "geometry": draw_geometry(jax.random.fold_in(keys[4], 71), 0),
    }


COURANT = 0.5
SPEED_EPS = 1e-06
RELAX = 0.5
MODULUS = 2.0
BETA = 0.5
VISCOSITY = 1.0
PENALTY = 20.0
LOWER = BETA
UPPER = BETA + PENALTY + 8.0 * VISCOSITY

def neighbour(values, axis, offset):
    widths = [(0, 0)] * values.ndim
    widths[axis] = (1, 1)
    padded = jnp.pad(values, widths)
    return lax.slice_in_dim(padded, 1 + offset, 1 + offset + values.shape[axis], axis=axis)

def centred(values, axis):
    return 0.5 * (neighbour(values, axis, 1) - neighbour(values, axis, -1))

def evolve(deviation, above, below, noise, flow_down, flow_across, gradients, time_step, noise_scale):
    last = deviation.ndim - 1
    left = neighbour(deviation, last, -1)
    right = neighbour(deviation, last, 1)
    advected = jnp.maximum(flow_down, 0.0) * (deviation - above) + jnp.minimum(flow_down, 0.0) * (below - deviation) + jnp.maximum(flow_across, 0.0) * (deviation - left) + jnp.minimum(flow_across, 0.0) * (right - deviation)
    down_down, down_across, across_down, across_across = gradients
    comp_down = deviation[0] + 1.0
    comp_shear = deviation[1]
    comp_across = deviation[2] + 1.0
    stretch = jnp.stack([2.0 * (down_down * comp_down + down_across * comp_shear), down_down * comp_shear + down_across * comp_across + comp_down * across_down + comp_shear * across_across, 2.0 * (across_down * comp_shear + across_across * comp_across)])
    return deviation + time_step * (stretch - advected - deviation / RELAX) + noise_scale * noise

def chebyshev(start, source, apply):
    centre = 0.5 * (UPPER + LOWER)
    radius = 0.5 * (UPPER - LOWER)
    sigma = centre / radius
    rho = 1.0 / sigma
    solution = start
    residual = source - apply(start)
    direction = residual / centre
    for index in range(ITERS):
        solution = solution + direction
        if index + 1 < ITERS:
            residual = residual - apply(direction)
            rho_next = 1.0 / (2.0 * sigma - rho)
            direction = rho_next * rho * direction + 2.0 * rho_next / radius * residual
            rho = rho_next
    return solution

def reference(fields, increments, velocity, geometry):
    speed_max = jnp.max(jnp.abs(velocity))
    time_step = COURANT / (speed_max + SPEED_EPS)
    noise_scale = jnp.sqrt(time_step / RELAX)
    flow_down = velocity[0]
    flow_across = velocity[1]
    gradients = (centred(flow_down, 0), centred(flow_down, 1), centred(flow_across, 0), centred(flow_across, 1))
    identity = jnp.array([1.0, 0.0, 1.0], jnp.float32).reshape(3, 1, 1)
    mask_values = geometry.astype(jnp.float32)

    def advance(index):
        deviation = lax.dynamic_index_in_dim(fields, index, 1, keepdims=False) - identity
        noise = lax.dynamic_index_in_dim(increments, index, 1, keepdims=False)
        above = neighbour(deviation, 1, -1)
        below = neighbour(deviation, 1, 1)
        return evolve(deviation, above, below, noise, flow_down, flow_across, gradients, time_step, noise_scale)
    new_deviation = lax.map(advance, jnp.arange(FIELDS, dtype=jnp.int32))
    stress = MODULUS / FIELDS * lax.optimization_barrier(jnp.sum(new_deviation * mask_values, axis=0))
    fields_new = jnp.moveaxis(new_deviation, 0, 1) + identity.reshape(3, 1, 1, 1)
    force = jnp.stack([centred(stress[0], 0) + centred(stress[1], 1), centred(stress[1], 0) + centred(stress[2], 1)])
    wall = PENALTY * (1.0 - mask_values)

    def apply(values):
        beside = neighbour(values, 1, 1) + neighbour(values, 1, -1) + neighbour(values, 2, 1) + neighbour(values, 2, -1)
        return (BETA + 4.0 * VISCOSITY + wall) * values - VISCOSITY * beside
    source = BETA * velocity + force
    velocity_new = chebyshev(velocity, source, apply)
    return (fields_new, velocity_new)
```

```python
import functools

import jax
import jax.numpy as jnp
from jax import lax
from jax.experimental import pallas as pl
from jax.experimental.pallas import tpu as pltpu
from jax.sharding import PartitionSpec as P

ITERS = 8
COURANT = 0.5
SPEED_EPS = 1e-06
RELAX = 0.5
MODULUS = 2.0
BETA = 0.5
VISCOSITY = 1.0
PENALTY = 20.0
LOWER = BETA
UPPER = BETA + PENALTY + 8.0 * VISCOSITY

MESH = pl.DeviceIdType.MESH
F32 = jnp.float32
LANES = 128
ROWS = 64
HALO = 8
TALL = ROWS + 2 * HALO
TILE = 64
TILES = 16
COLS = 8
FIELDS = 64
LOCAL = 4
RING = 4
PACKED = 72
SPLIT = 40
STRESS = 96
HALF = STRESS // 2
ORDER = (2, 1, 3, 0)


def slots():
    names = [("max", d) for d in range(1, 16)]
    names += [(n, d) for n in ("vrow", "frow", "own", "ownrow", "vcorner", "edge") for d in (0, 1)]
    names += [(n, o) for n in ("z", "zrow") for o in (1, 2, 3)]
    names += [("y", o, d) for o in (1, 2, 3) for d in (0, 1)]
    names += [("relay", o, d) for o in range(4) for d in (0, 1)]
    names += [(n, j, d) for n in ("half", "whole") for j in range(4) for d in (0, 1)]
    names += [("reduced", j) for j in range(3)]
    names += [("corner", a, b) for a in (0, 1) for b in (0, 1)]
    names += [("srow", d) for d in (0, 1)]
    return {name: at for at, name in enumerate(names)}


SLOTS = slots()


def kernel(
    fields, noise, velocity, geometry, fields_out, velocity_out,
    X, N, V, G, U, PG, M_own, M_all, VR_out, VR_in, FR_out, FR_in, VC_out, VC_in,
    Q, H_in, W_in, Z_in, T, E, B, B_in, E_in, local_sem, out_sem, send_sem, recv_sem,
):
    f = lax.axis_index("field")
    s = lax.axis_index("space")
    zh = f // RING
    y = f % RING
    right = zh * RING + (y + 1) % RING
    left = zh * RING + (y + RING - 1) % RING
    f_up, f_down = (f + 1) % TILES, (f + TILES - 1) % TILES
    s_up, s_down = (s + 1) % TILES, (s + TILES - 1) % TILES

    def z_peer(o):
        return (zh + o) % RING * RING + y

    def z_source(o):
        return (zh + RING - o) % RING * RING + y

    started = []

    def send(name, source, target, to_f, to_s):
        copy = pltpu.make_async_remote_copy(
            src_ref=source,
            dst_ref=target,
            send_sem=send_sem.at[SLOTS[name]],
            recv_sem=recv_sem.at[SLOTS[name]],
            device_id=(to_f, to_s),
            device_id_type=MESH,
        )
        copy.start()
        started.append(copy)

    def arrive(name, landed):
        pltpu.make_async_copy(landed, landed, recv_sem.at[SLOTS[name]]).wait()

    load_v = pltpu.make_async_copy(velocity, V, local_sem.at[0])
    load_v.start()
    load_g = pltpu.make_async_copy(geometry, G, local_sem.at[1])
    load_g.start()
    load_x, load_n = [], []
    for t in range(COLS):
        columns = slice(t * LANES, (t + 1) * LANES)
        load_x.append(
            pltpu.make_async_copy(
                fields.at[:, :, :, columns],
                X.at[:, :, t + 1, HALO : HALO + ROWS, :],
                local_sem.at[2 + t],
            )
        )
    for t in range(COLS):
        columns = slice(t * LANES, (t + 1) * LANES)
        load_n.append(
            pltpu.make_async_copy(
                noise.at[:, :, :, columns], N.at[:, :, t], local_sem.at[2 + COLS + t]
            )
        )
    for copy in load_x + load_n:
        copy.start()

    barrier = pltpu.get_barrier_semaphore()
    partners = [(f, (s + d) % TILES) for d in range(1, TILES)]
    partners += [(right, s), (left, s)]
    partners += [(z_peer(o), s) for o in (1, 2, 3)]
    partners += [(f_up, s), (f_down, s)]
    partners += [(a, b) for a in (f_up, f_down) for b in (s_up, s_down)]
    for partner in partners:
        pl.semaphore_signal(barrier, inc=1, device_id=partner, device_id_type=MESH)

    lane = lax.broadcasted_iota(jnp.int32, (8, LANES), 1)
    low = lane < TILE

    load_v.wait()
    own = jnp.concatenate([V[0], V[1]], axis=1)
    PG[f, 0:ROWS, :] = own
    M_own[...] = jnp.max(jnp.abs(own).reshape(ROWS // 8, 8, LANES), axis=0)
    VR_out[0, 0:8, :] = own[ROWS - 8 :]
    VR_out[1, 0:8, :] = own[0:8]

    load_g.wait()
    half = f % 2
    t_own = f // 2

    def walls(rows):
        def block(t):
            at = pl.multiple_of(jnp.clip(t, 0, COLS - 1) * LANES, LANES)
            return G[rows, pl.ds(at, LANES)].astype(F32)

        before, here, after = block(t_own - 1), block(t_own), block(t_own + 1)
        count = here.shape[0]
        at = lax.broadcasted_iota(jnp.int32, (count, LANES), 1)
        even = pltpu.roll(jnp.where(at < 120, here, before), HALO, axis=1)
        odd = pltpu.roll(jnp.where(at < HALO, after, here), HALO + TILE, axis=1)
        return jnp.where(half == 0, even, odd)

    VR_out[0, 8:16, :] = walls(slice(ROWS - 8, ROWS))
    VR_out[1, 8:16, :] = walls(slice(0, 8))

    pl.semaphore_wait(barrier, len(partners))

    main = PG.at[f, 0:ROWS]
    send(("own", 0), main, main, right, s)
    send(("own", 1), main, main, left, s)
    for o in (2, 1, 3):
        send(("z", o), main, main, z_peer(o), s)
    for d in range(1, TILES):
        send(("max", d), M_own, M_all.at[d], f, (s + d) % TILES)
    send(("vrow", 0), VR_out.at[0], VR_in.at[0], f, s_up)
    send(("vrow", 1), VR_out.at[1], VR_in.at[1], f, s_down)

    for copy in load_x:
        copy.wait()
    for c in range(3):
        for e in range(LOCAL):
            for t in range(COLS):
                FR_out[0, c * LOCAL + e, t : t + 1, :] = X[c, e, t + 1, HALO + ROWS - 1 : HALO + ROWS, :]
                FR_out[1, c * LOCAL + e, t : t + 1, :] = X[c, e, t + 1, HALO : HALO + 1, :]
    send(("frow", 0), FR_out.at[0], FR_in.at[0], f, s_up)
    send(("frow", 1), FR_out.at[1], FR_in.at[1], f, s_down)

    first, last = s == 0, s == TILES - 1
    for d in (0, 1):
        arrive(("vrow", d), VR_in.at[d])
    speed = M_own[...]
    for d in range(1, TILES):
        arrive(("max", d), M_all.at[d])
        speed = jnp.maximum(speed, M_all[d])
    speed = jnp.max(speed, axis=0, keepdims=True)
    above = jnp.where(first, 0.0, VR_in[0, 7:8, :])
    below = jnp.where(last, 0.0, VR_in[1, 0:1, :])
    PG[f, ROWS : ROWS + 1, :] = above
    PG[f, ROWS + 1 : ROWS + 2, :] = below
    PG[f, ROWS + 2 : PACKED, :] = jnp.broadcast_to(speed, (PACKED - ROWS - 2, LANES))
    rim = PG.at[f, ROWS:PACKED]
    send(("ownrow", 0), rim, rim, right, s)
    send(("ownrow", 1), rim, rim, left, s)
    for o in (2, 1, 3):
        send(("zrow", o), rim, rim, z_peer(o), s)
    VC_out[0:8, :] = VR_in[0, 0:8, :]
    VC_out[8:16, :] = VR_in[1, 0:8, :]
    send(("vcorner", 0), VC_out, VC_in.at[0], f_up, s)
    send(("vcorner", 1), VC_out, VC_in.at[1], f_down, s)

    def ring_tile(o, step):
        return (zh + RING - o) % RING * RING + (y + step) % RING

    def forward(o):
        tile = z_source(o)
        arrive(("z", o), PG.at[tile, 0:ROWS])
        arrive(("zrow", o), PG.at[tile, ROWS:PACKED])
        send(("y", o, 0), PG.at[tile], PG.at[tile], right, s)
        send(("y", o, 1), PG.at[tile], PG.at[tile], left, s)

    def relay(o):
        for d, step in ((0, RING - 1), (1, 1)):
            tile = ring_tile(o, step)
            if o == 0:
                arrive(("own", d), PG.at[tile, 0:ROWS])
                arrive(("ownrow", d), PG.at[tile, ROWS:PACKED])
            else:
                arrive(("y", o, d), PG.at[tile])
            part = PG.at[tile, 0:SPLIT] if d == 0 else PG.at[tile, SPLIT:PACKED]
            send(("relay", o, d), part, part, right if d == 0 else left, s)

    relay(0)
    forward(1)
    forward(3)
    relay(1)
    forward(2)
    relay(3)
    relay(2)

    for c in range(3):
        for e in range(LOCAL):
            for t in (0, COLS + 1):
                X[c, e, t, :, :] = jnp.full((TALL, LANES), float(c != 1), F32)
    for d in (0, 1):
        arrive(("frow", d), FR_in.at[d])
    for c in range(3):
        outside = float(c != 1)
        for e in range(LOCAL):
            row_above = jnp.where(first, outside, FR_in[0, c * LOCAL + e])
            row_below = jnp.where(last, outside, FR_in[1, c * LOCAL + e])
            for t in range(COLS):
                X[c, e, t + 1, HALO - 1 : HALO, :] = row_above[t : t + 1]
                X[c, e, t + 1, HALO + ROWS : HALO + ROWS + 1, :] = row_below[t : t + 1]
    for c in range(2):
        for t in (0, COLS + 1):
            U[c, t, :, :] = jnp.zeros((TALL, LANES), F32)
    for copy in load_n:
        copy.wait()

    for o in range(4):
        tile = ring_tile(o, 2)
        arrive(("relay", o, 0), PG.at[tile, 0:SPLIT])
        arrive(("relay", o, 1), PG.at[tile, SPLIT:PACKED])

    low_tile = lax.broadcasted_iota(jnp.int32, (PACKED, LANES), 1) < TILE

    def unpack(t, speed):
        even, odd = PG[2 * t], PG[2 * t + 1]
        u = jnp.where(low_tile, even, pltpu.roll(odd, TILE, axis=1))
        w = jnp.where(low_tile, pltpu.roll(even, TILE, axis=1), odd)
        for c, strip in ((0, u), (1, w)):
            U[c, t + 1, HALO : HALO + ROWS, :] = strip[0:ROWS]
            U[c, t + 1, HALO - 1 : HALO, :] = strip[ROWS : ROWS + 1]
            U[c, t + 1, HALO + ROWS : HALO + ROWS + 1, :] = strip[ROWS + 1 : ROWS + 2]
        return jnp.maximum(speed, jnp.maximum(even[ROWS + 2 : ROWS + 3], odd[ROWS + 2 : ROWS + 3]))

    speed = lax.fori_loop(0, COLS, unpack, jnp.zeros((1, LANES), F32))
    speed = jnp.max(speed, axis=1, keepdims=True)
    step = COURANT / (speed + SPEED_EPS)
    step = jnp.broadcast_to(step, (8, LANES))
    scale = jnp.sqrt(step / RELAX)

    at_first, at_last = lane == 0, lane == LANES - 1

    def beside(ref, lead, t, rows):
        here = ref[(*lead, t, rows, slice(None))]
        before = ref[(*lead, t - 1, rows, slice(None))]
        after = ref[(*lead, t + 1, rows, slice(None))]
        to_left = pltpu.roll(jnp.where(at_last, before, here), 1, axis=1)
        to_right = pltpu.roll(jnp.where(at_first, after, here), LANES - 1, axis=1)
        return here, to_left, to_right

    def advance(t, tt, row):
        rows = pl.ds(pl.multiple_of(row + HALO, 8), 8)
        rows_above = pl.ds(row + HALO - 1, 8)
        rows_below = pl.ds(row + HALO + 1, 8)
        strip = pl.ds(pl.multiple_of(row, 8), 8)
        u, u_left, u_right = beside(U, (0,), t, rows)
        w, w_left, w_right = beside(U, (1,), t, rows)
        half_step = 0.5 * step
        down_down = half_step * (U[0, t, rows_below, :] - U[0, t, rows_above, :])
        down_across = half_step * (u_right - u_left)
        across_down = half_step * (U[1, t, rows_below, :] - U[1, t, rows_above, :])
        across_across = half_step * (w_right - w_left)
        from_above = step * jnp.maximum(u, 0.0)
        from_below = -step * jnp.minimum(u, 0.0)
        from_left = step * jnp.maximum(w, 0.0)
        from_right = -step * jnp.minimum(w, 0.0)
        relaxed = step / RELAX
        kept = 1.0 - relaxed - (from_above + from_below) - (from_left + from_right)
        own_of = (
            kept + 2.0 * down_down,
            kept + (down_down + across_across),
            kept + 2.0 * across_across,
        )
        twice_across, twice_down = 2.0 * down_across, 2.0 * across_down
        total = [None, None, None]
        for e in range(LOCAL):
            here, new = [], []
            for c in range(3):
                x, x_left, x_right = beside(X, (c, e), t, rows)
                here.append(x)
                value = own_of[c] * x + scale * N[c, e, t - 1, strip, :]
                value += from_above * X[c, e, t, rows_above, :]
                value += from_below * X[c, e, t, rows_below, :]
                value += from_left * x_left + from_right * x_right
                new.append(value)
            new[0] += twice_across * here[1] + relaxed
            new[1] += down_across * here[2] + across_down * here[0]
            new[2] += twice_down * here[1] + relaxed
            for c in range(3):
                N[c, e, t - 1, strip, :] = new[c]
                total[c] = new[c] if e == 0 else total[c] + new[c]
        columns = pl.ds(pl.multiple_of((t - 1) * LANES, LANES), LANES)
        weight = MODULUS / FIELDS * G[strip, columns].astype(F32)
        return (
            weight * (total[0] - float(LOCAL)),
            weight * total[1],
            weight * (total[2] - float(LOCAL)),
        )

    def evolve(j):
        block = (zh + ORDER[j]) % RING

        def body(i, carry):
            tt, r = i // 4, i % 4
            t = 2 * block + tt + 1
            folded = []
            for part in (0, 1):
                row = (r + 4 * part) * 8
                xx, xy, yy = advance(t, tt, row)
                strip = pl.ds(pl.multiple_of(row, 8), 8)
                Q[j, 2 * tt, strip, :] = jnp.where(low, xx, pltpu.roll(xy, TILE, axis=1))
                Q[j, 2 * tt + 1, strip, :] = jnp.where(low, pltpu.roll(xx, TILE, axis=1), xy)
                folded.append(yy)
            strip = pl.ds(pl.multiple_of(r * 8 + ROWS, 8), 8)
            top, bottom = folded
            Q[j, 2 * tt, strip, :] = jnp.where(low, top, pltpu.roll(bottom, TILE, axis=1))
            Q[j, 2 * tt + 1, strip, :] = jnp.where(low, pltpu.roll(top, TILE, axis=1), bottom)
            return carry

        lax.fori_loop(0, 8, body, 0)
        stores = []
        for tt in (0, 1):
            t = 2 * block + tt
            columns = pl.ds(pl.multiple_of(t * LANES, LANES), LANES)
            store = pltpu.make_async_copy(
                N.at[:, :, t], fields_out.at[:, :, :, columns], out_sem.at[2 * j + tt]
            )
            store.start()
            stores.append(store)
        return stores

    y_up, y_down, y_far = (y + 1) % RING, (y + 3) % RING, (y + 2) % RING

    def ring_far(j):
        send(("half", j, 0), Q.at[j, y_far, 0:HALF], H_in.at[j, 0:HALF], right, s)
        send(("half", j, 1), Q.at[j, y_far, HALF:STRESS], H_in.at[j, HALF:STRESS], left, s)

    def ring_near(j):
        arrive(("half", j, 0), H_in.at[j, 0:HALF])
        Q[j, y_up, 0:HALF, :] += H_in[j, 0:HALF, :]
        send(("whole", j, 0), Q.at[j, y_up], W_in.at[j, 0], right, s)
        arrive(("half", j, 1), H_in.at[j, HALF:STRESS])
        Q[j, y_down, HALF:STRESS, :] += H_in[j, HALF:STRESS, :]
        send(("whole", j, 1), Q.at[j, y_down], W_in.at[j, 1], left, s)

    def ring_sum(j):
        arrive(("whole", j, 0), W_in.at[j, 0])
        arrive(("whole", j, 1), W_in.at[j, 1])
        T[j] = Q[j, y] + (W_in[j, 0] + W_in[j, 1])
        if ORDER[j]:
            send(("reduced", j), T.at[j], Z_in.at[j], z_peer(ORDER[j]), s)

    stores = []
    for j in range(4):
        stores += evolve(j)
        ring_far(j)
        if j >= 1:
            ring_near(j - 1)
        if j >= 2:
            ring_sum(j - 2)
    ring_near(3)
    ring_sum(2)

    at_row = lax.broadcasted_iota(jnp.int32, (TALL, LANES), 0) + (s * ROWS - HALO)
    at_lane = lax.broadcasted_iota(jnp.int32, (TALL, LANES), 1)
    at_col = at_lane + (f * TILE - HALO)
    inside = (at_row >= 0) & (at_row < TILES * ROWS) & (at_col >= 0) & (at_col < TILES * TILE)
    inside = inside & (at_lane < TALL)
    for d in (0, 1):
        arrive(("vcorner", d), VC_in.at[d])

    def stacked(rim_rows, tile):
        return jnp.concatenate([rim_rows[0:8], PG[tile, 0:ROWS, :], rim_rows[8:16]], axis=0)

    v_mid = stacked(VC_out, f)
    v_left = stacked(VC_in.at[0], f_down)
    v_right = stacked(VC_in.at[1], f_up)

    def window(before, here, after):
        return jnp.where(at_lane < HALO, before, jnp.where(at_lane < HALO + TILE, here, after))

    near = lambda v: pltpu.roll(v, HALO, axis=1)
    far = lambda v: pltpu.roll(v, HALO + TILE, axis=1)
    speeds = (
        jnp.where(inside, window(far(v_left), near(v_mid), far(v_right)), 0.0),
        jnp.where(inside, window(near(v_left), far(v_mid), near(v_right)), 0.0),
    )
    mask = jnp.concatenate([VR_in[0, 8:16, :], walls(slice(0, ROWS)), VR_in[1, 8:16, :]], axis=0)
    weight = BETA + 4.0 * VISCOSITY + PENALTY * (1.0 - mask)

    def around(values):
        return (
            pltpu.roll(values, TALL - 1, axis=0)
            + pltpu.roll(values, 1, axis=0)
            + pltpu.roll(values, LANES - 1, axis=1)
            + pltpu.roll(values, 1, axis=1)
        )

    def apply(values):
        return weight * values - VISCOSITY * around(values)

    ring_sum(3)
    total = T[3]
    for j in range(3):
        arrive(("reduced", j), Z_in.at[j])
        total = total + Z_in[j]
    xx_xy, yy = total[0:ROWS], total[ROWS:STRESS]
    tile_stress = (near(xx_xy), far(xx_xy), jnp.concatenate([near(yy), far(yy)], axis=0))
    edges = jnp.zeros((ROWS, LANES), F32)
    at_edge = lax.broadcasted_iota(jnp.int32, (ROWS, LANES), 1)
    for c in range(3):
        E[c, :, :] = tile_stress[c]
        low_edge = pltpu.roll(tile_stress[c], LANES - TILE + 8 * c, axis=1)
        high_edge = pltpu.roll(tile_stress[c], 16 + 8 * c, axis=1)
        edges = jnp.where((at_edge >= 8 * c) & (at_edge < 8 * c + 8), low_edge, edges)
        edges = jnp.where((at_edge >= 24 + 8 * c) & (at_edge < 32 + 8 * c), high_edge, edges)
    B[...] = edges
    for a, to_f in ((0, f_up), (1, f_down)):
        send(("edge", a), B, B_in.at[a, HALO : HALO + ROWS], to_f, s)
    for b, to_s in ((0, s_up), (1, s_down)):
        rows = slice(ROWS - 8, ROWS) if b == 0 else slice(0, 8)
        send(("srow", b), E.at[:, rows], E_in.at[b], f, to_s)
        for a, to_f in ((0, f_up), (1, f_down)):
            landing = slice(0, 8) if b == 0 else slice(HALO + ROWS, TALL)
            send(("corner", a, b), B.at[rows], B_in.at[a, landing], to_f, to_s)

    residual = [BETA * v - apply(v) for v in speeds]

    for b in (0, 1):
        arrive(("srow", b), E_in.at[b])
        for a in (0, 1):
            landing = slice(0, 8) if b == 0 else slice(HALO + ROWS, TALL)
            arrive(("corner", a, b), B_in.at[a, landing])
    for a in (0, 1):
        arrive(("edge", a), B_in.at[a, HALO : HALO + ROWS])
    stress = []
    for c in range(3):
        middle = jnp.concatenate([E_in[0, c], E[c], E_in[1, c]], axis=0)
        before = pltpu.roll(B_in[0], (LANES - 8 * c) % LANES, axis=1)
        after = pltpu.roll(B_in[1], 48 - 8 * c, axis=1)
        stress.append(jnp.where(inside, window(before, middle, after), 0.0))

    def along_rows(values):
        return pltpu.roll(values, TALL - 1, axis=0) - pltpu.roll(values, 1, axis=0)

    def along_cols(values):
        return pltpu.roll(values, LANES - 1, axis=1) - pltpu.roll(values, 1, axis=1)

    force = (
        0.5 * (along_rows(stress[0]) + along_cols(stress[1])),
        0.5 * (along_rows(stress[1]) + along_cols(stress[2])),
    )
    centre = 0.5 * (UPPER + LOWER)
    radius = 0.5 * (UPPER - LOWER)
    sigma = centre / radius
    for c in range(2):
        rho = 1.0 / sigma
        v = speeds[c]
        r = jnp.where(inside, residual[c] + force[c], 0.0)
        d = r / centre
        for index in range(ITERS):
            v = v + d
            if index + 1 < ITERS:
                r = jnp.where(inside, r - apply(d), 0.0)
                rho_next = 1.0 / (2.0 * sigma - rho)
                d = rho_next * rho * d + 2.0 * rho_next / radius * r
                rho = rho_next
        velocity_out[c, :, :] = pltpu.roll(v, LANES - HALO, axis=1)[HALO : HALO + ROWS, 0:TILE]

    for copy in started:
        copy.wait_send()
    for store in stores:
        store.wait()


def per_device(fields, increments, velocity, geometry):
    anywhere = pl.BlockSpec(memory_space=pl.ANY)

    def vmem(*shape):
        return pltpu.VMEM(shape, F32)

    return pl.pallas_call(
        kernel,
        out_shape=(
            jax.ShapeDtypeStruct(fields.shape, F32),
            jax.ShapeDtypeStruct(velocity.shape, F32),
        ),
        in_specs=[anywhere] * 4,
        out_specs=(anywhere, pl.BlockSpec(memory_space=pltpu.VMEM)),
        scratch_shapes=[
            vmem(3, LOCAL, COLS + 2, TALL, LANES),
            vmem(3, LOCAL, COLS, ROWS, LANES),
            vmem(2, ROWS, TILE),
            pltpu.VMEM((ROWS, COLS * LANES), jnp.int32),
            vmem(2, COLS + 2, TALL, LANES),
            vmem(TILES, PACKED, LANES),
            vmem(8, LANES),
            vmem(TILES, 8, LANES),
            vmem(2, 16, LANES),
            vmem(2, 16, LANES),
            vmem(2, 3 * LOCAL, COLS, LANES),
            vmem(2, 3 * LOCAL, COLS, LANES),
            vmem(16, LANES),
            vmem(2, 16, LANES),
            vmem(RING, RING, STRESS, LANES),
            vmem(RING, STRESS, LANES),
            vmem(RING, 2, STRESS, LANES),
            vmem(3, STRESS, LANES),
            vmem(RING, STRESS, LANES),
            vmem(3, ROWS, LANES),
            vmem(ROWS, LANES),
            vmem(2, TALL, LANES),
            vmem(2, 3, 8, LANES),
            pltpu.SemaphoreType.DMA((2 + 2 * COLS,)),
            pltpu.SemaphoreType.DMA((COLS,)),
            pltpu.SemaphoreType.DMA((len(SLOTS),)),
            pltpu.SemaphoreType.DMA((len(SLOTS),)),
        ],
        compiler_params=pltpu.CompilerParams(
            collective_id=0, has_side_effects=True, vmem_limit_bytes=40 * 1024 * 1024
        ),
        name="step",
    )(fields, increments, velocity, geometry)


def solution(mesh):
    placed = (
        P(None, "field", "space", None),
        P(None, "field", "space", None),
        P(None, "space", "field"),
        P("space", None),
    )
    return jax.shard_map(
        per_device,
        mesh=mesh,
        in_specs=placed,
        out_specs=(P(None, "field", "space", None), P(None, "space", "field")),
        check_vma=False,
    )
```

```python
import functools

import jax
import jax.numpy as jnp
from jax import lax
from jax.experimental import pallas as pl
from jax.experimental.pallas import tpu as pltpu
from jax.sharding import PartitionSpec as P

ITERS = 8
COURANT = 0.5
SPEED_EPS = 1e-06
RELAX = 0.5
MODULUS = 2.0
BETA = 0.5
VISCOSITY = 1.0
PENALTY = 20.0
LOWER = BETA
UPPER = BETA + PENALTY + 8.0 * VISCOSITY

MESH = pl.DeviceIdType.MESH
F32 = jnp.float32
LANES = 128
ROWS = 64
HALO = 8
TALL = ROWS + 2 * HALO
TILE = 64
TILES = 16
COLS = 8
FIELDS = 64
LOCAL = 4
VMEM_LIMIT = 63 * 1024 * 1024
RING = 4
PACKED = 72
EDGE = 12 * 3 + 1


def slots():
    names = [(n, d) for n in ("max", "rim") for d in range(1, 16)]
    names += [(n, d) for n in ("vrow", "frow", "vcorner", "side", "end") for d in (0, 1)]
    names += [(n, d) for n in ("z", "y") for d in (1, 2, 3)]
    names += [("zy", o, d) for o in (1, 2, 3) for d in (1, 2, 3)]
    names += [("part", j, d) for j in range(4) for d in (1, 2, 3)]
    names += [("sum", j) for j in range(3)]
    names += [("corner", a, b) for a in (0, 1) for b in (0, 1)]
    return {name: at for at, name in enumerate(names)}


SLOTS = slots()


def coefficients(step, u, w):
    (u, u_above, u_below, u_left, u_right), (w, w_above, w_below, w_left, w_right) = u, w
    half_step = 0.5 * step
    down_down = half_step * (u_below - u_above)
    down_across = half_step * (u_right - u_left)
    across_down = half_step * (w_below - w_above)
    across_across = half_step * (w_right - w_left)
    from_above = step * jnp.maximum(u, 0.0)
    from_below = -step * jnp.minimum(u, 0.0)
    from_left = step * jnp.maximum(w, 0.0)
    from_right = -step * jnp.minimum(w, 0.0)
    relaxed = step / RELAX
    kept = 1.0 - relaxed - (from_above + from_below) - (from_left + from_right)
    own = (
        kept + 2.0 * down_down,
        kept + (down_down + across_across),
        kept + 2.0 * across_across,
    )
    return own, (from_above, from_below, from_left, from_right), down_across, across_down, relaxed


def update(weights, scale, tensors, noises):
    own, sides, down_across, across_down, relaxed = weights
    new = []
    for c in range(3):
        value = own[c] * tensors[c][0] + scale * noises[c]
        for side, beside in zip(sides, tensors[c][1:]):
            value = value + side * beside
        new.append(value)
    xx, xy, yy = (tensor[0] for tensor in tensors)
    return (
        new[0] + (2.0 * down_across * xy + relaxed),
        new[1] + (down_across * yy + across_down * xx),
        new[2] + (2.0 * across_down * xy + relaxed),
    )


def kernel(
    fields, noise, velocity, geometry, fields_out, velocity_out,
    X, N, V, G, U, UE, S, PG, M_own, M_all, VR_out, VR_in, FE_out, FE_in, VC_out, VC_in,
    Q, Y_in, Z_in, T, F, F_in, E_in, local_sem, send_sem, recv_sem,
):
    f = lax.axis_index("field")
    s = lax.axis_index("space")
    zh = f // RING
    y = f % RING
    f_up, f_down = (f + 1) % TILES, (f + TILES - 1) % TILES
    s_up, s_down = (s + 1) % TILES, (s + TILES - 1) % TILES
    first, last = s == 0, s == TILES - 1

    def y_peer(d):
        return zh * RING + (y + d) % RING

    def z_peer(o):
        return (zh + o) % RING * RING + y

    def peer_back(o, d):
        return (zh + RING - o) % RING * RING + (y + RING - d) % RING

    started = []

    def send(name, source, target, to_f, to_s):
        copy = pltpu.make_async_remote_copy(
            src_ref=source,
            dst_ref=target,
            send_sem=send_sem.at[SLOTS[name]],
            recv_sem=recv_sem.at[SLOTS[name]],
            device_id=(to_f, to_s),
            device_id_type=MESH,
        )
        copy.start()
        started.append(copy)

    def arrive(name, landed):
        pltpu.make_async_copy(landed, landed, recv_sem.at[SLOTS[name]]).wait()

    barrier = pltpu.get_barrier_semaphore()
    partners = [(f, (s + d) % TILES) for d in range(1, TILES)]
    partners += [((f + d) % TILES, s) for d in range(1, TILES)]
    partners += [(a, b) for a in (f_up, f_down) for b in (s_up, s_down)]
    for partner in partners:
        pl.semaphore_signal(barrier, inc=1, device_id=partner, device_id_type=MESH)

    load_v = pltpu.make_async_copy(velocity, V, local_sem.at[0])
    load_v.start()
    load_g = pltpu.make_async_copy(geometry, G, local_sem.at[1])
    load_g.start()
    loads = []
    for c in range(3):
        inner = X.at[c, :, HALO : HALO + ROWS, LANES : LANES + COLS * LANES]
        loads.append(pltpu.make_async_copy(fields.at[c], inner, local_sem.at[2 + c]))
    for c in range(3):
        loads.append(pltpu.make_async_copy(noise.at[c], N.at[c], local_sem.at[5 + c]))
    for copy in loads:
        copy.start()

    lane = lax.broadcasted_iota(jnp.int32, (8, LANES), 1)
    row = lax.broadcasted_iota(jnp.int32, (8, LANES), 0)
    low = lane < TILE
    at_left, at_right = lane == 0, lane == LANES - 1
    at_top, at_bottom = row == 0, row == 7

    load_v.wait()
    own = jnp.concatenate([V[0], V[1]], axis=1)
    PG[f, 0:ROWS, :] = own
    M_own[...] = jnp.max(jnp.abs(own).reshape(ROWS // 8, 8, LANES), axis=0)
    VR_out[0, 0:8, :] = own[ROWS - 8 :]
    VR_out[1, 0:8, :] = own[0:8]

    load_g.wait()
    half = f % 2
    t_own = f // 2

    def walls(rows):
        def block(t):
            at = pl.multiple_of(jnp.clip(t, 0, COLS - 1) * LANES, LANES)
            return G[rows, pl.ds(at, LANES)].astype(F32)

        before, here, after = block(t_own - 1), block(t_own), block(t_own + 1)
        count = here.shape[0]
        at = lax.broadcasted_iota(jnp.int32, (count, LANES), 1)
        even = pltpu.roll(jnp.where(at < 120, here, before), HALO, axis=1)
        odd = pltpu.roll(jnp.where(at < HALO, after, here), HALO + TILE, axis=1)
        return jnp.where(half == 0, even, odd)

    VR_out[0, 8:16, :] = walls(slice(ROWS - 8, ROWS))
    VR_out[1, 8:16, :] = walls(slice(0, 8))

    pl.semaphore_wait(barrier, len(partners))

    main = PG.at[f, 0:ROWS]
    for o in (2, 1, 3):
        send(("z", o), main, main, z_peer(o), s)
    for d in (2, 1, 3):
        send(("y", d), main, main, y_peer(d), s)
    send(("vrow", 0), VR_out.at[0], VR_in.at[0], f, s_up)
    send(("vrow", 1), VR_out.at[1], VR_in.at[1], f, s_down)
    for d in range(1, TILES):
        send(("max", d), M_own, M_all.at[d], f, (s + d) % TILES)

    for copy in loads:
        copy.wait()
    for t in range(COLS):
        columns = slice(t * LANES, (t + 1) * LANES)
        inner = slice((t + 1) * LANES, (t + 2) * LANES)
        here = slice(t, t + 1)
        for c in range(3):
            for e in range(LOCAL):
                at = c * LOCAL + e
                for side, edge, step in ((0, ROWS - 1, -1), (1, 0, 1)):
                    near = HALO + edge
                    FE_out[side, at, here, :] = X[c, e, near : near + 1, inner]
                    FE_out[side, 12 + at, here, :] = X[c, e, near + step : near + step + 1, inner]
                    FE_out[side, 24 + at, here, :] = N[c, e, edge : edge + 1, columns]
        for side, edge in ((0, ROWS - 1), (1, 0)):
            FE_out[side, EDGE - 1, here, :] = G[edge : edge + 1, columns].astype(F32)
    send(("frow", 0), FE_out.at[0], FE_in.at[0], f, s_up)
    send(("frow", 1), FE_out.at[1], FE_in.at[1], f, s_down)

    for d in (0, 1):
        arrive(("vrow", d), VR_in.at[d])
    speed = M_own[...]
    for d in range(1, TILES):
        arrive(("max", d), M_all.at[d])
        speed = jnp.maximum(speed, M_all[d])
    speed = jnp.max(speed, axis=0, keepdims=True)
    above = jnp.where(first, 0.0, VR_in[0, 6:8, :])
    below = jnp.where(last, 0.0, VR_in[1, 0:2, :])
    PG[f, ROWS : ROWS + 2, :] = above
    PG[f, ROWS + 2 : ROWS + 4, :] = below
    PG[f, ROWS + 4 : PACKED, :] = jnp.broadcast_to(speed, (PACKED - ROWS - 4, LANES))
    rim = PG.at[f, ROWS:PACKED]
    for d in range(1, TILES):
        send(("rim", d), rim, rim, (f + d) % TILES, s)

    for o in (1, 3, 2):
        tile = PG.at[peer_back(o, 0), 0:ROWS]
        arrive(("z", o), tile)
        for d in (2, 1, 3):
            send(("zy", o, d), tile, tile, y_peer(d), s)
    VC_out[0:8, :] = VR_in[0, 0:8, :]
    VC_out[8:16, :] = VR_in[1, 0:8, :]
    send(("vcorner", 0), VC_out, VC_in.at[0], f_up, s)
    send(("vcorner", 1), VC_out, VC_in.at[1], f_down, s)

    for c in range(3):
        for e in range(LOCAL):
            for t in (0, COLS + 1):
                outer = slice(t * LANES, (t + 1) * LANES)
                X[c, e, :, outer] = jnp.full((TALL, LANES), float(c != 1), F32)
    for t in (0, COLS + 1):
        U[:, :, t * LANES : (t + 1) * LANES] = jnp.zeros((2, TALL, LANES), F32)
        S[:, t, :, :] = jnp.zeros((3, TALL, LANES), F32)
    for d in (0, 1):
        arrive(("frow", d), FE_in.at[d])
    for c in range(3):
        outside = float(c != 1)
        for e in range(LOCAL):
            row_above = jnp.where(first, outside, FE_in[0, c * LOCAL + e])
            row_below = jnp.where(last, outside, FE_in[1, c * LOCAL + e])
            for t in range(COLS):
                inner = slice((t + 1) * LANES, (t + 2) * LANES)
                X[c, e, HALO - 1 : HALO, inner] = row_above[t : t + 1]
                X[c, e, HALO + ROWS : HALO + ROWS + 1, inner] = row_below[t : t + 1]

    for d in (1, 2, 3):
        arrive(("y", d), PG.at[peer_back(0, d), 0:ROWS])
    for o in (1, 3, 2):
        for d in (1, 2, 3):
            arrive(("zy", o, d), PG.at[peer_back(o, d), 0:ROWS])
    for d in range(1, TILES):
        arrive(("rim", d), PG.at[(f + TILES - d) % TILES, ROWS:PACKED])

    low_tile = lax.broadcasted_iota(jnp.int32, (PACKED, LANES), 1) < TILE
    speed = jnp.zeros((1, LANES), F32)
    for t in range(COLS):
        even, odd = PG[2 * t], PG[2 * t + 1]
        u = jnp.where(low_tile, even, pltpu.roll(odd, TILE, axis=1))
        w = jnp.where(low_tile, pltpu.roll(even, TILE, axis=1), odd)
        columns = slice((t + 1) * LANES, (t + 2) * LANES)
        here = slice(t, t + 1)
        for c, strip in ((0, u), (1, w)):
            U[c, HALO : HALO + ROWS, columns] = strip[0:ROWS]
            U[c, HALO - 2 : HALO, columns] = strip[ROWS : ROWS + 2]
            U[c, HALO + ROWS : HALO + ROWS + 2, columns] = strip[ROWS + 2 : ROWS + 4]
            UE[0, c, 0, here, :] = strip[ROWS + 1 : ROWS + 2]
            UE[0, c, 1, here, :] = strip[ROWS : ROWS + 1]
            UE[0, c, 2, here, :] = strip[0:1]
            UE[1, c, 0, here, :] = strip[ROWS + 2 : ROWS + 3]
            UE[1, c, 1, here, :] = strip[ROWS - 1 : ROWS]
            UE[1, c, 2, here, :] = strip[ROWS + 3 : ROWS + 4]
        speed = jnp.maximum(speed, jnp.maximum(even[ROWS + 4 : ROWS + 5], odd[ROWS + 4 : ROWS + 5]))
    speed = jnp.max(speed, axis=1, keepdims=True)
    step = COURANT / (speed + SPEED_EPS)
    step = jnp.broadcast_to(step, (8, LANES))
    scale = jnp.sqrt(step / RELAX)

    def stress_of(total, weight):
        weight = MODULUS / FIELDS * weight
        return (
            weight * (total[0] - float(LOCAL)),
            weight * total[1],
            weight * (total[2] - float(LOCAL)),
        )

    def added(total, new):
        return new if total is None else tuple(a + b for a, b in zip(total, new))

    def spread(centre, above, below, outside):
        to_right = pltpu.roll(centre, 1, axis=1)
        to_left = pltpu.roll(centre, LANES - 1, axis=1)
        before = jnp.where(at_top, outside, pltpu.roll(to_right, 1, axis=0))
        after = jnp.where(at_bottom, outside, pltpu.roll(to_left, 7, axis=0))
        left = jnp.where(at_left, before, to_right)
        right = jnp.where(at_right, after, to_left)
        return centre, above, below, left, right

    for side, absent, place in ((0, first, HALO - 1), (1, last, HALO + ROWS)):
        weights = coefficients(step, *(spread(*(UE[side, c, q] for q in range(3)), 0.0) for c in range(2)))
        total = None
        for e in range(LOCAL):
            tensors = []
            for c in range(3):
                at = c * LOCAL + e
                centre, outer, inner = FE_in[side, at], FE_in[side, 12 + at], FE_out[1 - side, at]
                above, below = (outer, inner) if side == 0 else (inner, outer)
                tensors.append(spread(centre, above, below, float(c != 1)))
            noises = [FE_in[side, 24 + c * LOCAL + e] for c in range(3)]
            total = added(total, update(weights, scale, tensors, noises))
        for c, values in enumerate(stress_of(total, FE_in[side, EDGE - 1])):
            values = jnp.where(absent, 0.0, values)
            for t in range(COLS):
                S[c, t + 1, place : place + 1, :] = values[t : t + 1]

    def block_at(t):
        return pl.ds(pl.multiple_of(t * LANES, LANES), LANES)

    def nearby(ref, lead, r, t):
        rows, columns = pl.ds(pl.multiple_of(r * 8 + HALO, 8), 8), block_at(t)
        rows_above = pl.ds(pl.multiple_of(r * 8, 8), 8)
        rows_below = pl.ds(pl.multiple_of(r * 8 + 2 * HALO, 8), 8)
        here = ref[(*lead, rows, columns)]
        above = jnp.where(at_bottom, ref[(*lead, rows_above, columns)], here)
        below = jnp.where(at_top, ref[(*lead, rows_below, columns)], here)
        left = jnp.where(at_right, ref[(*lead, rows, block_at(t - 1))], here)
        right = jnp.where(at_left, ref[(*lead, rows, block_at(t + 1))], here)
        return (
            here,
            pltpu.roll(above, 1, axis=0),
            pltpu.roll(below, 7, axis=0),
            pltpu.roll(left, 1, axis=1),
            pltpu.roll(right, LANES - 1, axis=1),
        )

    start = 2 * ((zh + 1) % RING) + COLS - 1

    def advance(i, carry):
        t = (start + i // 8) % COLS + 1
        r = i % 8
        rows, columns = pl.ds(pl.multiple_of(r * 8, 8), 8), block_at(t - 1)
        weights = coefficients(step, nearby(U, (0,), r, t), nearby(U, (1,), r, t))
        total = None
        for e in range(LOCAL):
            tensors = [nearby(X, (c, e), r, t) for c in range(3)]
            noises = [N[c, e, rows, columns] for c in range(3)]
            new = update(weights, scale, tensors, noises)
            for c in range(3):
                N[c, e, rows, columns] = new[c]
            total = added(total, new)
        weight = G[rows, columns].astype(F32)
        for c, values in enumerate(stress_of(total, weight)):
            S[c, t, pl.ds(pl.multiple_of(r * 8 + HALO, 8), 8), :] = values
        return carry

    def forces(j):
        block = (zh + 1 + j) % RING

        def body(i, carry):
            tt, r = i // 8, i % 8
            t = 2 * block + tt + 1
            rows = pl.ds(pl.multiple_of(r * 8 + HALO, 8), 8)

            def along_rows(c):
                return S[c, t, pl.ds(r * 8 + HALO + 1, 8), :] - S[c, t, pl.ds(r * 8 + HALO - 1, 8), :]

            def along_cols(c):
                here = S[c, t, rows, :]
                left = jnp.where(at_right, S[c, t - 1, rows, :], here)
                right = jnp.where(at_left, S[c, t + 1, rows, :], here)
                return pltpu.roll(right, LANES - 1, axis=1) - pltpu.roll(left, 1, axis=1)

            down = 0.5 * (along_rows(0) + along_cols(1))
            across = 0.5 * (along_rows(1) + along_cols(2))
            rows = pl.ds(pl.multiple_of(r * 8, 8), 8)
            Q[j, 2 * tt, rows, :] = jnp.where(low, down, pltpu.roll(across, TILE, axis=1))
            Q[j, 2 * tt + 1, rows, :] = jnp.where(low, pltpu.roll(down, TILE, axis=1), across)
            return carry

        lax.fori_loop(0, 16, body, 0)
        for d in (2, 1, 3):
            send(("part", j, d), Q.at[j, (y + d) % RING], Y_in.at[j, d - 1], y_peer(d), s)

    def ring_sum(j):
        for d in (1, 2, 3):
            arrive(("part", j, d), Y_in.at[j, d - 1])
        T[j] = (Q[j, y] + Y_in[j, 0]) + (Y_in[j, 1] + Y_in[j, 2])
        if j < 3:
            send(("sum", j), T.at[j], Z_in.at[j], z_peer(j + 1), s)

    lax.fori_loop(0, 32, advance, 0)
    forces(0)
    lax.fori_loop(32, 48, advance, 0)
    forces(1)
    lax.fori_loop(48, 64, advance, 0)
    forces(2)
    forces(3)
    store = pltpu.make_async_copy(N, fields_out, local_sem.at[8])
    store.start()
    ring_sum(0)
    ring_sum(1)
    ring_sum(2)

    at_row = lax.broadcasted_iota(jnp.int32, (TALL, LANES), 0) + (s * ROWS - HALO)
    at_lane = lax.broadcasted_iota(jnp.int32, (TALL, LANES), 1)
    at_col = at_lane + (f * TILE - HALO)
    inside = (at_row >= 0) & (at_row < TILES * ROWS) & (at_col >= 0) & (at_col < TILES * TILE)
    inside = inside & (at_lane < TALL)
    for d in (0, 1):
        arrive(("vcorner", d), VC_in.at[d])

    def windows(before, here, after):
        near = lambda v: pltpu.roll(v, HALO, axis=1)
        far = lambda v: pltpu.roll(v, HALO + TILE, axis=1)

        def window(a, b, c):
            joined = jnp.where(at_lane < HALO, a, jnp.where(at_lane < HALO + TILE, b, c))
            return jnp.where(inside, joined, 0.0)

        return (
            window(far(before), near(here), far(after)),
            window(near(before), far(here), near(after)),
        )

    def stacked(rim_rows, tile):
        return jnp.concatenate([rim_rows[0:8], PG[tile, 0:ROWS, :], rim_rows[8:16]], axis=0)

    speeds = windows(
        stacked(VC_in.at[0], f_down), stacked(VC_out, f), stacked(VC_in.at[1], f_up)
    )
    mask = jnp.concatenate([VR_in[0, 8:16, :], walls(slice(0, ROWS)), VR_in[1, 8:16, :]], axis=0)
    weight = BETA + 4.0 * VISCOSITY + PENALTY * (1.0 - mask)

    def apply(values):
        around = (
            pltpu.roll(values, TALL - 1, axis=0)
            + pltpu.roll(values, 1, axis=0)
            + pltpu.roll(values, LANES - 1, axis=1)
            + pltpu.roll(values, 1, axis=1)
        )
        return weight * values - VISCOSITY * around

    residual = [BETA * v - apply(v) for v in speeds]

    ring_sum(3)
    total = T[3]
    for j in range(3):
        arrive(("sum", j), Z_in.at[j])
        total = total + Z_in[j]
    F[...] = total
    for b, to_s in ((0, s_up), (1, s_down)):
        rows = slice(ROWS - 8, ROWS) if b == 0 else slice(0, 8)
        landing = slice(0, 8) if b == 0 else slice(HALO + ROWS, TALL)
        for a, to_f in ((0, f_up), (1, f_down)):
            send(("corner", a, b), F.at[rows], F_in.at[a, landing], to_f, to_s)
    for a, to_f in ((0, f_up), (1, f_down)):
        send(("side", a), F, F_in.at[a, HALO : HALO + ROWS], to_f, s)
    for b, to_s in ((0, s_up), (1, s_down)):
        rows = slice(ROWS - 8, ROWS) if b == 0 else slice(0, 8)
        send(("end", b), F.at[rows], E_in.at[b], f, to_s)
    for b in (0, 1):
        arrive(("end", b), E_in.at[b])
    for a in (0, 1):
        arrive(("side", a), F_in.at[a, HALO : HALO + ROWS])
    for b in (0, 1):
        for a in (0, 1):
            landing = slice(0, 8) if b == 0 else slice(HALO + ROWS, TALL)
            arrive(("corner", a, b), F_in.at[a, landing])
    force = windows(F_in[0], jnp.concatenate([E_in[0], F[...], E_in[1]], axis=0), F_in[1])

    centre = 0.5 * (UPPER + LOWER)
    radius = 0.5 * (UPPER - LOWER)
    sigma = centre / radius
    for c in range(2):
        rho = 1.0 / sigma
        v = speeds[c]
        r = jnp.where(inside, residual[c] + force[c], 0.0)
        d = r / centre
        for index in range(ITERS):
            v = v + d
            if index + 1 < ITERS:
                r = jnp.where(inside, r - apply(d), 0.0)
                rho_next = 1.0 / (2.0 * sigma - rho)
                d = rho_next * rho * d + 2.0 * rho_next / radius * r
                rho = rho_next
        velocity_out[c, :, :] = pltpu.roll(v, LANES - HALO, axis=1)[HALO : HALO + ROWS, 0:TILE]

    for copy in started:
        copy.wait_send()
    store.wait()


def per_device(fields, increments, velocity, geometry):
    hbm = pl.BlockSpec(memory_space=pltpu.HBM)

    def vmem(*shape):
        return pltpu.VMEM(shape, F32)

    return pl.pallas_call(
        kernel,
        out_shape=(
            jax.ShapeDtypeStruct(fields.shape, F32),
            jax.ShapeDtypeStruct(velocity.shape, F32),
        ),
        in_specs=[hbm] * 4,
        out_specs=(hbm, pl.BlockSpec(memory_space=pltpu.VMEM)),
        scratch_shapes=[
            vmem(3, LOCAL, TALL, (COLS + 2) * LANES),
            vmem(3, LOCAL, ROWS, COLS * LANES),
            vmem(2, ROWS, TILE),
            pltpu.VMEM((ROWS, COLS * LANES), jnp.int32),
            vmem(2, TALL, (COLS + 2) * LANES),
            vmem(2, 2, 3, COLS, LANES),
            vmem(3, COLS + 2, TALL, LANES),
            vmem(TILES, PACKED, LANES),
            vmem(8, LANES),
            vmem(TILES, 8, LANES),
            vmem(2, 16, LANES),
            vmem(2, 16, LANES),
            vmem(2, EDGE, COLS, LANES),
            vmem(2, EDGE, COLS, LANES),
            vmem(16, LANES),
            vmem(2, 16, LANES),
            vmem(RING, RING, ROWS, LANES),
            vmem(RING, 3, ROWS, LANES),
            vmem(3, ROWS, LANES),
            vmem(RING, ROWS, LANES),
            vmem(ROWS, LANES),
            vmem(2, TALL, LANES),
            vmem(2, 8, LANES),
            pltpu.SemaphoreType.DMA((9,)),
            pltpu.SemaphoreType.DMA((len(SLOTS),)),
            pltpu.SemaphoreType.DMA((len(SLOTS),)),
        ],
        compiler_params=pltpu.CompilerParams(
            collective_id=0, has_side_effects=True, vmem_limit_bytes=VMEM_LIMIT
        ),
        name="step",
    )(fields, increments, velocity, geometry)


def solution(mesh):
    placed = (
        P(None, "field", "space", None),
        P(None, "field", "space", None),
        P(None, "space", "field"),
        P("space", None),
    )
    return jax.shard_map(
        per_device,
        mesh=mesh,
        in_specs=placed,
        out_specs=(P(None, "field", "space", None), P(None, "space", "field")),
        check_vma=False,
    )
```

```python
import functools

import jax
import jax.numpy as jnp
from jax import lax
from jax.experimental import pallas as pl
from jax.experimental.pallas import tpu as pltpu
from jax.sharding import PartitionSpec as P

ITERS = 8
COURANT = 0.5
SPEED_EPS = 1e-06
RELAX = 0.5
MODULUS = 2.0
BETA = 0.5
VISCOSITY = 1.0
PENALTY = 20.0
LOWER = BETA
UPPER = BETA + PENALTY + 8.0 * VISCOSITY

MESH = pl.DeviceIdType.MESH
F32 = jnp.float32
LANES = 128
ROWS = 64
HALO = 8
TALL = ROWS + 2 * HALO
TILE = 64
TILES = 16
COLS = 8
FIELDS = 64
LOCAL = 4
VMEM_LIMIT = 63 * 1024 * 1024
RING = 4
CHUNKS = 2
PIECE = ROWS // CHUNKS
PACKED = 72
EDGE = 12 * 3 + 1


def slots():
    names = [(n, d) for n in ("max", "rim") for d in range(1, 16)]
    names += [(n, d) for n in ("vrow", "frow", "vcorner", "side", "end") for d in (0, 1)]
    names += [("y", d) for d in (1, 2, 3)]
    names += [("z", o, h) for o in (1, 2, 3) for h in range(CHUNKS)]
    names += [("zy", o, d, h) for o in (1, 2, 3) for d in (1, 2, 3) for h in range(CHUNKS)]
    names += [("part", j, d) for j in range(4) for d in (1, 2, 3)]
    names += [("sum", j) for j in range(3)]
    names += [("corner", a, b) for a in (0, 1) for b in (0, 1)]
    return {name: at for at, name in enumerate(names)}


SLOTS = slots()


def coefficients(step, u, w):
    (u, u_above, u_below, u_left, u_right), (w, w_above, w_below, w_left, w_right) = u, w
    half_step = 0.5 * step
    down_down = half_step * (u_below - u_above)
    down_across = half_step * (u_right - u_left)
    across_down = half_step * (w_below - w_above)
    across_across = half_step * (w_right - w_left)
    down, across = step * jnp.abs(u), step * jnp.abs(w)
    relaxed = step * (1.0 / RELAX)
    kept = 1.0 - relaxed - down - across
    own = (
        kept + 2.0 * down_down,
        kept + (down_down + across_across),
        kept + 2.0 * across_across,
    )
    return own, (u > 0.0, w > 0.0), (down, across), down_across, across_down, relaxed


def update(weights, scale, tensors, noises):
    own, (downward, rightward), (down, across), down_across, across_down, relaxed = weights
    new = []
    for c in range(3):
        here, above, below, left, right = tensors[c]
        upwind = down * jnp.where(downward, above, below)
        sidewind = across * jnp.where(rightward, left, right)
        new.append((own[c] * here + scale * noises[c]) + (upwind + sidewind))
    xx, xy, yy = (tensor[0] for tensor in tensors)
    return (
        new[0] + (2.0 * down_across * xy + relaxed),
        new[1] + (down_across * yy + across_down * xx),
        new[2] + (2.0 * across_down * xy + relaxed),
    )


def kernel(
    fields, noise, velocity, geometry, fields_out, velocity_out,
    XN, XC, XL, XR, N, V, G, U, UE, S, PG, M_own, M_all, VR_out, VR_in, FE_out, FE_in, VC_out, VC_in,
    Q, Y_in, Z_in, T, F, F_in, E_in, local_sem, send_sem, recv_sem,
):
    f = lax.axis_index("field")
    s = lax.axis_index("space")
    zh = f // RING
    y = f % RING
    f_up, f_down = (f + 1) % TILES, (f + TILES - 1) % TILES
    s_up, s_down = (s + 1) % TILES, (s + TILES - 1) % TILES
    first, last = s == 0, s == TILES - 1

    def y_peer(d):
        return zh * RING + (y + d) % RING

    def z_peer(o):
        return (zh + o) % RING * RING + y

    def peer_back(o, d):
        return (zh + RING - o) % RING * RING + (y + RING - d) % RING

    started = []

    def send(name, source, target, to_f, to_s):
        copy = pltpu.make_async_remote_copy(
            src_ref=source,
            dst_ref=target,
            send_sem=send_sem.at[SLOTS[name]],
            recv_sem=recv_sem.at[SLOTS[name]],
            device_id=(to_f, to_s),
            device_id_type=MESH,
        )
        copy.start()
        started.append(copy)

    def arrive(name, landed):
        pltpu.make_async_copy(landed, landed, recv_sem.at[SLOTS[name]]).wait()

    barrier = pltpu.get_barrier_semaphore()
    partners = [(f, (s + d) % TILES) for d in range(1, TILES)]
    partners += [((f + d) % TILES, s) for d in range(1, TILES)]
    partners += [(a, b) for a in (f_up, f_down) for b in (s_up, s_down)]
    for partner in partners:
        pl.semaphore_signal(barrier, inc=1, device_id=partner, device_id_type=MESH)

    load_v = pltpu.make_async_copy(velocity, V, local_sem.at[0])
    load_v.start()
    load_g = pltpu.make_async_copy(geometry, G, local_sem.at[1])
    load_g.start()
    loads = []
    for c in range(3):
        loads.append(pltpu.make_async_copy(fields.at[c], XN.at[c], local_sem.at[2 + c]))
    for c in range(3):
        loads.append(pltpu.make_async_copy(noise.at[c], N.at[c], local_sem.at[5 + c]))
    for copy in loads:
        copy.start()

    lane = lax.broadcasted_iota(jnp.int32, (8, LANES), 1)
    row = lax.broadcasted_iota(jnp.int32, (8, LANES), 0)
    low = lane < TILE
    at_left, at_right = lane == 0, lane == LANES - 1
    at_top, at_bottom = row == 0, row == 7

    load_v.wait()
    own = jnp.concatenate([V[0], V[1]], axis=1)
    PG[f, 0:ROWS, :] = own
    M_own[...] = jnp.max(jnp.abs(own).reshape(ROWS // 8, 8, LANES), axis=0)
    VR_out[0, 0:8, :] = own[ROWS - 8 :]
    VR_out[1, 0:8, :] = own[0:8]

    load_g.wait()
    half = f % 2
    t_own = f // 2

    def walls(rows):
        def block(t):
            at = pl.multiple_of(jnp.clip(t, 0, COLS - 1) * LANES, LANES)
            return G[rows, pl.ds(at, LANES)].astype(F32)

        before, here, after = block(t_own - 1), block(t_own), block(t_own + 1)
        count = here.shape[0]
        at = lax.broadcasted_iota(jnp.int32, (count, LANES), 1)
        even = pltpu.roll(jnp.where(at < 120, here, before), HALO, axis=1)
        odd = pltpu.roll(jnp.where(at < HALO, after, here), HALO + TILE, axis=1)
        return jnp.where(half == 0, even, odd)

    VR_out[0, 8:16, :] = walls(slice(ROWS - 8, ROWS))
    VR_out[1, 8:16, :] = walls(slice(0, 8))

    pl.semaphore_wait(barrier, len(partners))

    main = PG.at[f, 0:ROWS]
    for h in range(CHUNKS):
        piece = PG.at[f, h * PIECE : (h + 1) * PIECE]
        for o in (2, 1, 3):
            send(("z", o, h), piece, piece, z_peer(o), s)
    for d in (2, 1, 3):
        send(("y", d), main, main, y_peer(d), s)
    send(("vrow", 0), VR_out.at[0], VR_in.at[0], f, s_up)
    send(("vrow", 1), VR_out.at[1], VR_in.at[1], f, s_down)
    for d in range(1, TILES):
        send(("max", d), M_own, M_all.at[d], f, (s + d) % TILES)

    for copy in loads:
        copy.wait()
    for t in range(COLS):
        columns = slice(t * LANES, (t + 1) * LANES)
        here = slice(t, t + 1)
        for c in range(3):
            for e in range(LOCAL):
                at = c * LOCAL + e
                for side, edge, step in ((0, ROWS - 1, -1), (1, 0, 1)):
                    second = edge + step
                    FE_out[side, at, here, :] = XN[c, e, edge : edge + 1, columns]
                    FE_out[side, 12 + at, here, :] = XN[c, e, second : second + 1, columns]
                    FE_out[side, 24 + at, here, :] = N[c, e, edge : edge + 1, columns]
        for side, edge in ((0, ROWS - 1), (1, 0)):
            FE_out[side, EDGE - 1, here, :] = G[edge : edge + 1, columns].astype(F32)
    send(("frow", 0), FE_out.at[0], FE_in.at[0], f, s_up)
    send(("frow", 1), FE_out.at[1], FE_in.at[1], f, s_down)

    for d in (0, 1):
        arrive(("vrow", d), VR_in.at[d])
    speed = M_own[...]
    for d in range(1, TILES):
        arrive(("max", d), M_all.at[d])
        speed = jnp.maximum(speed, M_all[d])
    speed = jnp.max(speed, axis=0, keepdims=True)
    above = jnp.where(first, 0.0, VR_in[0, 6:8, :])
    below = jnp.where(last, 0.0, VR_in[1, 0:2, :])
    PG[f, ROWS : ROWS + 2, :] = above
    PG[f, ROWS + 2 : ROWS + 4, :] = below
    PG[f, ROWS + 4 : PACKED, :] = jnp.broadcast_to(speed, (PACKED - ROWS - 4, LANES))
    rim = PG.at[f, ROWS:PACKED]
    for d in range(1, TILES):
        send(("rim", d), rim, rim, (f + d) % TILES, s)

    for h in range(CHUNKS):
        for o in (1, 3, 2):
            piece = PG.at[peer_back(o, 0), h * PIECE : (h + 1) * PIECE]
            arrive(("z", o, h), piece)
            for d in (2, 1, 3):
                send(("zy", o, d, h), piece, piece, y_peer(d), s)
    VC_out[0:8, :] = VR_in[0, 0:8, :]
    VC_out[8:16, :] = VR_in[1, 0:8, :]
    send(("vcorner", 0), VC_out, VC_in.at[0], f_up, s)
    send(("vcorner", 1), VC_out, VC_in.at[1], f_down, s)

    def block_at(t):
        return pl.ds(pl.multiple_of(t * LANES, LANES), LANES)

    def prepare(i, carry):
        t, r = i // 8, i % 8
        rows, rows_in = pl.ds(pl.multiple_of(r * 8, 8), 8), pl.ds(pl.multiple_of(r * 8 + HALO, 8), 8)
        here_at, before_at = block_at(t), block_at(jnp.maximum(t - 1, 0))
        after_at = block_at(jnp.minimum(t + 1, COLS - 1))
        for c in range(3):
            outside = float(c != 1)
            for e in range(LOCAL):
                here = XN[c, e, rows, here_at]
                before = jnp.where(t == 0, outside, XN[c, e, rows, before_at])
                after = jnp.where(t == COLS - 1, outside, XN[c, e, rows, after_at])
                XC[c, e, t, rows_in, :] = here
                XL[c, e, t, rows, :] = pltpu.roll(jnp.where(at_right, before, here), 1, axis=1)
                XR[c, e, t, rows, :] = pltpu.roll(jnp.where(at_left, after, here), LANES - 1, axis=1)
        return carry

    lax.fori_loop(0, 64, prepare, 0)
    for t in (0, COLS + 1):
        U[:, :, t * LANES : (t + 1) * LANES] = jnp.zeros((2, TALL, LANES), F32)
        S[:, t, :, :] = jnp.zeros((3, TALL, LANES), F32)
    for d in (0, 1):
        arrive(("frow", d), FE_in.at[d])
    for c in range(3):
        outside = float(c != 1)
        for e in range(LOCAL):
            row_above = jnp.where(first, outside, FE_in[0, c * LOCAL + e])
            row_below = jnp.where(last, outside, FE_in[1, c * LOCAL + e])
            for t in range(COLS):
                XC[c, e, t, HALO - 1 : HALO, :] = row_above[t : t + 1]
                XC[c, e, t, HALO + ROWS : HALO + ROWS + 1, :] = row_below[t : t + 1]

    for d in (1, 2, 3):
        arrive(("y", d), PG.at[peer_back(0, d), 0:ROWS])
    for o in (1, 3, 2):
        for d in (1, 2, 3):
            for h in range(CHUNKS):
                arrive(("zy", o, d, h), PG.at[peer_back(o, d), h * PIECE : (h + 1) * PIECE])
    for d in range(1, TILES):
        arrive(("rim", d), PG.at[(f + TILES - d) % TILES, ROWS:PACKED])

    low_tile = lax.broadcasted_iota(jnp.int32, (PACKED, LANES), 1) < TILE
    speed = jnp.zeros((1, LANES), F32)
    for t in range(COLS):
        even, odd = PG[2 * t], PG[2 * t + 1]
        u = jnp.where(low_tile, even, pltpu.roll(odd, TILE, axis=1))
        w = jnp.where(low_tile, pltpu.roll(even, TILE, axis=1), odd)
        columns = slice((t + 1) * LANES, (t + 2) * LANES)
        here = slice(t, t + 1)
        for c, strip in ((0, u), (1, w)):
            U[c, HALO : HALO + ROWS, columns] = strip[0:ROWS]
            U[c, HALO - 2 : HALO, columns] = strip[ROWS : ROWS + 2]
            U[c, HALO + ROWS : HALO + ROWS + 2, columns] = strip[ROWS + 2 : ROWS + 4]
            UE[0, c, 0, here, :] = strip[ROWS + 1 : ROWS + 2]
            UE[0, c, 1, here, :] = strip[ROWS : ROWS + 1]
            UE[0, c, 2, here, :] = strip[0:1]
            UE[1, c, 0, here, :] = strip[ROWS + 2 : ROWS + 3]
            UE[1, c, 1, here, :] = strip[ROWS - 1 : ROWS]
            UE[1, c, 2, here, :] = strip[ROWS + 3 : ROWS + 4]
        speed = jnp.maximum(speed, jnp.maximum(even[ROWS + 4 : ROWS + 5], odd[ROWS + 4 : ROWS + 5]))
    speed = jnp.max(speed, axis=1, keepdims=True)
    step = COURANT / (speed + SPEED_EPS)
    step = jnp.broadcast_to(step, (8, LANES))
    scale = jnp.sqrt(step / RELAX)

    def stress_of(total, weight):
        weight = MODULUS / FIELDS * weight
        return (
            weight * (total[0] - float(LOCAL)),
            weight * total[1],
            weight * (total[2] - float(LOCAL)),
        )

    def added(total, new):
        return new if total is None else tuple(a + b for a, b in zip(total, new))

    def spread(centre, above, below, outside):
        to_right = pltpu.roll(centre, 1, axis=1)
        to_left = pltpu.roll(centre, LANES - 1, axis=1)
        before = jnp.where(at_top, outside, pltpu.roll(to_right, 1, axis=0))
        after = jnp.where(at_bottom, outside, pltpu.roll(to_left, 7, axis=0))
        left = jnp.where(at_left, before, to_right)
        right = jnp.where(at_right, after, to_left)
        return centre, above, below, left, right

    for side, absent, place in ((0, first, HALO - 1), (1, last, HALO + ROWS)):
        weights = coefficients(step, *(spread(*(UE[side, c, q] for q in range(3)), 0.0) for c in range(2)))
        total = None
        for e in range(LOCAL):
            tensors = []
            for c in range(3):
                at = c * LOCAL + e
                centre, outer, inner = FE_in[side, at], FE_in[side, 12 + at], FE_out[1 - side, at]
                above, below = (outer, inner) if side == 0 else (inner, outer)
                tensors.append(spread(centre, above, below, float(c != 1)))
            noises = [FE_in[side, 24 + c * LOCAL + e] for c in range(3)]
            total = added(total, update(weights, scale, tensors, noises))
        for c, values in enumerate(stress_of(total, FE_in[side, EDGE - 1])):
            values = jnp.where(absent, 0.0, values)
            for t in range(COLS):
                S[c, t + 1, place : place + 1, :] = values[t : t + 1]

    def nearby(ref, lead, r, t):
        rows, columns = pl.ds(pl.multiple_of(r * 8 + HALO, 8), 8), block_at(t)
        rows_above = pl.ds(pl.multiple_of(r * 8, 8), 8)
        rows_below = pl.ds(pl.multiple_of(r * 8 + 2 * HALO, 8), 8)
        here = ref[(*lead, rows, columns)]
        above = jnp.where(at_bottom, ref[(*lead, rows_above, columns)], here)
        below = jnp.where(at_top, ref[(*lead, rows_below, columns)], here)
        left = jnp.where(at_right, ref[(*lead, rows, block_at(t - 1))], here)
        right = jnp.where(at_left, ref[(*lead, rows, block_at(t + 1))], here)
        return (
            here,
            pltpu.roll(above, 1, axis=0),
            pltpu.roll(below, 7, axis=0),
            pltpu.roll(left, 1, axis=1),
            pltpu.roll(right, LANES - 1, axis=1),
        )

    start = 2 * ((zh + 1) % RING) + COLS - 1

    def advance(i, carry):
        t = (start + i // 4) % COLS
        for part in (0, 1):
            r = i % 4 * 2 + part
            rows, columns = pl.ds(pl.multiple_of(r * 8, 8), 8), block_at(t)
            rows_in = pl.ds(pl.multiple_of(r * 8 + HALO, 8), 8)
            rows_above, rows_below = pl.ds(r * 8 + HALO - 1, 8), pl.ds(r * 8 + HALO + 1, 8)
            weights = coefficients(step, nearby(U, (0,), r, t + 1), nearby(U, (1,), r, t + 1))
            total = None
            for e in range(LOCAL):
                tensors = [
                    (
                        XC[c, e, t, rows_in, :],
                        XC[c, e, t, rows_above, :],
                        XC[c, e, t, rows_below, :],
                        XL[c, e, t, rows, :],
                        XR[c, e, t, rows, :],
                    )
                    for c in range(3)
                ]
                noises = [N[c, e, rows, columns] for c in range(3)]
                new = update(weights, scale, tensors, noises)
                for c in range(3):
                    N[c, e, rows, columns] = new[c]
                total = added(total, new)
            weight = G[rows, columns].astype(F32)
            for c, values in enumerate(stress_of(total, weight)):
                S[c, t + 1, rows_in, :] = values
        return carry

    def forces(j):
        block = (zh + 1 + j) % RING

        def body(tt, carry):
            t = 2 * block + tt + 1
            for r in range(ROWS // 8):
                top = r * 8 + HALO
                rows = slice(top, top + 8)

                def along_rows(c):
                    return S[c, t, top + 1 : top + 9, :] - S[c, t, top - 1 : top + 7, :]

                def along_cols(c):
                    here = S[c, t, rows, :]
                    left = jnp.where(at_right, S[c, t - 1, rows, :], here)
                    right = jnp.where(at_left, S[c, t + 1, rows, :], here)
                    return pltpu.roll(right, LANES - 1, axis=1) - pltpu.roll(left, 1, axis=1)

                down = 0.5 * (along_rows(0) + along_cols(1))
                across = 0.5 * (along_rows(1) + along_cols(2))
                packed = slice(r * 8, r * 8 + 8)
                Q[j, 2 * tt, packed, :] = jnp.where(low, down, pltpu.roll(across, TILE, axis=1))
                Q[j, 2 * tt + 1, packed, :] = jnp.where(low, pltpu.roll(down, TILE, axis=1), across)
            return carry

        lax.fori_loop(0, 2, body, 0)
        for d in (2, 1, 3):
            send(("part", j, d), Q.at[j, (y + d) % RING], Y_in.at[j, d - 1], y_peer(d), s)

    def ring_sum(j):
        for d in (1, 2, 3):
            arrive(("part", j, d), Y_in.at[j, d - 1])
        T[j] = (Q[j, y] + Y_in[j, 0]) + (Y_in[j, 1] + Y_in[j, 2])
        if j < 3:
            send(("sum", j), T.at[j], Z_in.at[j], z_peer(j + 1), s)

    lax.fori_loop(0, 16, advance, 0)
    forces(0)
    lax.fori_loop(16, 24, advance, 0)
    forces(1)
    lax.fori_loop(24, 32, advance, 0)
    forces(2)
    forces(3)
    store = pltpu.make_async_copy(N, fields_out, local_sem.at[8])
    store.start()
    ring_sum(0)
    ring_sum(1)
    ring_sum(2)

    at_row = lax.broadcasted_iota(jnp.int32, (TALL, LANES), 0) + (s * ROWS - HALO)
    at_lane = lax.broadcasted_iota(jnp.int32, (TALL, LANES), 1)
    at_col = at_lane + (f * TILE - HALO)
    inside = (at_row >= 0) & (at_row < TILES * ROWS) & (at_col >= 0) & (at_col < TILES * TILE)
    inside = inside & (at_lane < TALL)
    for d in (0, 1):
        arrive(("vcorner", d), VC_in.at[d])

    def windows(before, here, after):
        near = lambda v: pltpu.roll(v, HALO, axis=1)
        far = lambda v: pltpu.roll(v, HALO + TILE, axis=1)

        def window(a, b, c):
            joined = jnp.where(at_lane < HALO, a, jnp.where(at_lane < HALO + TILE, b, c))
            return jnp.where(inside, joined, 0.0)

        return (
            window(far(before), near(here), far(after)),
            window(near(before), far(here), near(after)),
        )

    def stacked(rim_rows, tile):
        return jnp.concatenate([rim_rows[0:8], PG[tile, 0:ROWS, :], rim_rows[8:16]], axis=0)

    speeds = windows(
        stacked(VC_in.at[0], f_down), stacked(VC_out, f), stacked(VC_in.at[1], f_up)
    )
    mask = jnp.concatenate([VR_in[0, 8:16, :], walls(slice(0, ROWS)), VR_in[1, 8:16, :]], axis=0)
    weight = BETA + 4.0 * VISCOSITY + PENALTY * (1.0 - mask)

    def apply(values):
        around = (
            pltpu.roll(values, TALL - 1, axis=0)
            + pltpu.roll(values, 1, axis=0)
            + pltpu.roll(values, LANES - 1, axis=1)
            + pltpu.roll(values, 1, axis=1)
        )
        return weight * values - VISCOSITY * around

    residual = [BETA * v - apply(v) for v in speeds]

    ring_sum(3)
    total = T[3]
    for j in range(3):
        arrive(("sum", j), Z_in.at[j])
        total = total + Z_in[j]
    F[...] = total
    for b, to_s in ((0, s_up), (1, s_down)):
        rows = slice(ROWS - 8, ROWS) if b == 0 else slice(0, 8)
        landing = slice(0, 8) if b == 0 else slice(HALO + ROWS, TALL)
        for a, to_f in ((0, f_up), (1, f_down)):
            send(("corner", a, b), F.at[rows], F_in.at[a, landing], to_f, to_s)
    for a, to_f in ((0, f_up), (1, f_down)):
        send(("side", a), F, F_in.at[a, HALO : HALO + ROWS], to_f, s)
    for b, to_s in ((0, s_up), (1, s_down)):
        rows = slice(ROWS - 8, ROWS) if b == 0 else slice(0, 8)
        send(("end", b), F.at[rows], E_in.at[b], f, to_s)
    for b in (0, 1):
        arrive(("end", b), E_in.at[b])
    for a in (0, 1):
        arrive(("side", a), F_in.at[a, HALO : HALO + ROWS])
    for b in (0, 1):
        for a in (0, 1):
            landing = slice(0, 8) if b == 0 else slice(HALO + ROWS, TALL)
            arrive(("corner", a, b), F_in.at[a, landing])
    force = windows(F_in[0], jnp.concatenate([E_in[0], F[...], E_in[1]], axis=0), F_in[1])

    centre = 0.5 * (UPPER + LOWER)
    radius = 0.5 * (UPPER - LOWER)
    sigma = centre / radius
    for c in range(2):
        rho = 1.0 / sigma
        v = speeds[c]
        r = jnp.where(inside, residual[c] + force[c], 0.0)
        d = r / centre
        for index in range(ITERS):
            v = v + d
            if index + 1 < ITERS:
                r = jnp.where(inside, r - apply(d), 0.0)
                rho_next = 1.0 / (2.0 * sigma - rho)
                d = rho_next * rho * d + 2.0 * rho_next / radius * r
                rho = rho_next
        velocity_out[c, :, :] = pltpu.roll(v, LANES - HALO, axis=1)[HALO : HALO + ROWS, 0:TILE]

    for copy in started:
        copy.wait_send()
    store.wait()


def per_device(fields, increments, velocity, geometry):
    hbm = pl.BlockSpec(memory_space=pltpu.HBM)

    def vmem(*shape):
        return pltpu.VMEM(shape, F32)

    return pl.pallas_call(
        kernel,
        out_shape=(
            jax.ShapeDtypeStruct(fields.shape, F32),
            jax.ShapeDtypeStruct(velocity.shape, F32),
        ),
        in_specs=[hbm] * 4,
        out_specs=(hbm, pl.BlockSpec(memory_space=pltpu.VMEM)),
        scratch_shapes=[
            vmem(3, LOCAL, ROWS, COLS * LANES),
            vmem(3, LOCAL, COLS, TALL, LANES),
            vmem(3, LOCAL, COLS, ROWS, LANES),
            vmem(3, LOCAL, COLS, ROWS, LANES),
            vmem(3, LOCAL, ROWS, COLS * LANES),
            vmem(2, ROWS, TILE),
            pltpu.VMEM((ROWS, COLS * LANES), jnp.int32),
            vmem(2, TALL, (COLS + 2) * LANES),
            vmem(2, 2, 3, COLS, LANES),
            vmem(3, COLS + 2, TALL, LANES),
            vmem(TILES, PACKED, LANES),
            vmem(8, LANES),
            vmem(TILES, 8, LANES),
            vmem(2, 16, LANES),
            vmem(2, 16, LANES),
            vmem(2, EDGE, COLS, LANES),
            vmem(2, EDGE, COLS, LANES),
            vmem(16, LANES),
            vmem(2, 16, LANES),
            vmem(RING, RING, ROWS, LANES),
            vmem(RING, 3, ROWS, LANES),
            vmem(3, ROWS, LANES),
            vmem(RING, ROWS, LANES),
            vmem(ROWS, LANES),
            vmem(2, TALL, LANES),
            vmem(2, 8, LANES),
            pltpu.SemaphoreType.DMA((9,)),
            pltpu.SemaphoreType.DMA((len(SLOTS),)),
            pltpu.SemaphoreType.DMA((len(SLOTS),)),
        ],
        compiler_params=pltpu.CompilerParams(
            collective_id=0, has_side_effects=True, vmem_limit_bytes=VMEM_LIMIT
        ),
        name="step",
    )(fields, increments, velocity, geometry)


def solution(mesh):
    placed = (
        P(None, "field", "space", None),
        P(None, "field", "space", None),
        P(None, "space", "field"),
        P("space", None),
    )
    return jax.shard_map(
        per_device,
        mesh=mesh,
        in_specs=placed,
        out_specs=(P(None, "field", "space", None), P(None, "space", "field")),
        check_vma=False,
    )
```

```python
import functools

import jax
import jax.numpy as jnp
from jax import lax
from jax.experimental import pallas as pl
from jax.experimental.pallas import tpu as pltpu
from jax.sharding import PartitionSpec as P

ITERS = 8
COURANT = 0.5
SPEED_EPS = 1e-06
RELAX = 0.5
MODULUS = 2.0
BETA = 0.5
VISCOSITY = 1.0
PENALTY = 20.0
LOWER = BETA
UPPER = BETA + PENALTY + 8.0 * VISCOSITY

MESH = pl.DeviceIdType.MESH
F32 = jnp.float32
LANES = 128
ROWS = 64
HALO = 8
TALL = ROWS + 2 * HALO
TILE = 64
TILES = 16
COLS = 8
FIELDS = 64
LOCAL = 4
VMEM_LIMIT = 63 * 1024 * 1024
RING = 4
CHUNKS = 2
PIECE = ROWS // CHUNKS
PACKED = 72
EDGE = 12 * 3 + 1


def slots():
    names = [(n, d) for n in ("max", "rim") for d in range(1, 16)]
    names += [(n, d) for n in ("vrow", "frow", "vcorner") for d in (0, 1)]
    names += [("y", d) for d in (1, 2, 3)]
    names += [("z", o, h) for o in (1, 2, 3) for h in range(CHUNKS)]
    names += [("zy", o, d, h) for o in (1, 2, 3) for d in (1, 2, 3) for h in range(CHUNKS)]
    names += [("part", j, d) for j in range(4) for d in (1, 2, 3)]
    names += [("sum", j) for j in range(3)]
    names += [(n, d, j) for n in ("side", "end") for d in (0, 1) for j in range(4)]
    names += [("corner", a, b, j) for a in (0, 1) for b in (0, 1) for j in range(4)]
    return {name: at for at, name in enumerate(names)}


SLOTS = slots()


def coefficients(step, u, w):
    (u, u_above, u_below, u_left, u_right), (w, w_above, w_below, w_left, w_right) = u, w
    half_step = 0.5 * step
    down_down = half_step * (u_below - u_above)
    down_across = half_step * (u_right - u_left)
    across_down = half_step * (w_below - w_above)
    across_across = half_step * (w_right - w_left)
    down, across = step * jnp.abs(u), step * jnp.abs(w)
    relaxed = step * (1.0 / RELAX)
    kept = 1.0 - relaxed - down - across
    own = (
        kept + 2.0 * down_down,
        kept + (down_down + across_across),
        kept + 2.0 * across_across,
    )
    return own, (u > 0.0, w > 0.0), (down, across), down_across, across_down, relaxed


def update(weights, scale, tensors, noises):
    own, (downward, rightward), (down, across), down_across, across_down, relaxed = weights
    new = []
    for c in range(3):
        here, above, below, left, right = tensors[c]
        upwind = down * jnp.where(downward, above, below)
        sidewind = across * jnp.where(rightward, left, right)
        new.append((own[c] * here + scale * noises[c]) + (upwind + sidewind))
    xx, xy, yy = (tensor[0] for tensor in tensors)
    return (
        new[0] + (2.0 * down_across * xy + relaxed),
        new[1] + (down_across * yy + across_down * xx),
        new[2] + (2.0 * across_down * xy + relaxed),
    )


def kernel(
    fields, noise, velocity, geometry, fields_out, velocity_out,
    XN, XC, XL, XR, N, V, G, U, UE, S, PG, M_own, M_all, VR_out, VR_in, FE_out, FE_in, VC_out, VC_in,
    Q, Y_in, Z_in, T, C, C_in, E_in, K_in, local_sem, send_sem, recv_sem,
):
    f = lax.axis_index("field")
    s = lax.axis_index("space")
    zh = f // RING
    y = f % RING
    f_up, f_down = (f + 1) % TILES, (f + TILES - 1) % TILES
    s_up, s_down = (s + 1) % TILES, (s + TILES - 1) % TILES
    first, last = s == 0, s == TILES - 1

    def y_peer(d):
        return zh * RING + (y + d) % RING

    def z_peer(o):
        return (zh + o) % RING * RING + y

    def peer_back(o, d):
        return (zh + RING - o) % RING * RING + (y + RING - d) % RING

    started = []

    def send(name, source, target, to_f, to_s):
        copy = pltpu.make_async_remote_copy(
            src_ref=source,
            dst_ref=target,
            send_sem=send_sem.at[SLOTS[name]],
            recv_sem=recv_sem.at[SLOTS[name]],
            device_id=(to_f, to_s),
            device_id_type=MESH,
        )
        copy.start()
        started.append(copy)

    def arrive(name, landed):
        pltpu.make_async_copy(landed, landed, recv_sem.at[SLOTS[name]]).wait()

    barrier = pltpu.get_barrier_semaphore()
    partners = [(f, (s + d) % TILES) for d in range(1, TILES)]
    partners += [((f + d) % TILES, s) for d in range(1, TILES)]
    partners += [(z_peer(o), b) for o in (1, 2, 3) for b in (s_up, s_down)]
    partners += [
        ((z_peer(o) + a) % TILES, b) for o in range(4) for a in (1, TILES - 1) for b in (s_up, s_down)
    ]
    for partner in partners:
        pl.semaphore_signal(barrier, inc=1, device_id=partner, device_id_type=MESH)

    load_v = pltpu.make_async_copy(velocity, V, local_sem.at[0])
    load_v.start()
    load_g = pltpu.make_async_copy(geometry, G, local_sem.at[1])
    load_g.start()
    loads = []
    for c in range(3):
        loads.append(pltpu.make_async_copy(fields.at[c], XN.at[c], local_sem.at[2 + c]))
    for c in range(3):
        loads.append(pltpu.make_async_copy(noise.at[c], N.at[c], local_sem.at[5 + c]))
    for copy in loads:
        copy.start()

    lane = lax.broadcasted_iota(jnp.int32, (8, LANES), 1)
    row = lax.broadcasted_iota(jnp.int32, (8, LANES), 0)
    low = lane < TILE
    at_left, at_right = lane == 0, lane == LANES - 1
    at_top, at_bottom = row == 0, row == 7

    load_v.wait()
    own = jnp.concatenate([V[0], V[1]], axis=1)
    PG[f, 0:ROWS, :] = own
    M_own[...] = jnp.max(jnp.abs(own).reshape(ROWS // 8, 8, LANES), axis=0)
    VR_out[0, 0:8, :] = own[ROWS - 8 :]
    VR_out[1, 0:8, :] = own[0:8]

    load_g.wait()
    half = f % 2
    t_own = f // 2

    def walls(rows):
        def block(t):
            at = pl.multiple_of(jnp.clip(t, 0, COLS - 1) * LANES, LANES)
            return G[rows, pl.ds(at, LANES)].astype(F32)

        before, here, after = block(t_own - 1), block(t_own), block(t_own + 1)
        count = here.shape[0]
        at = lax.broadcasted_iota(jnp.int32, (count, LANES), 1)
        even = pltpu.roll(jnp.where(at < 120, here, before), HALO, axis=1)
        odd = pltpu.roll(jnp.where(at < HALO, after, here), HALO + TILE, axis=1)
        return jnp.where(half == 0, even, odd)

    VR_out[0, 8:16, :] = walls(slice(ROWS - 8, ROWS))
    VR_out[1, 8:16, :] = walls(slice(0, 8))

    pl.semaphore_wait(barrier, len(partners))

    send(("vrow", 0), VR_out.at[0], VR_in.at[0], f, s_up)
    send(("vrow", 1), VR_out.at[1], VR_in.at[1], f, s_down)
    for d in range(1, TILES):
        send(("max", d), M_own, M_all.at[d], f, (s + d) % TILES)
    main = PG.at[f, 0:ROWS]
    for h in range(CHUNKS):
        piece = PG.at[f, h * PIECE : (h + 1) * PIECE]
        for o in (2, 1, 3):
            send(("z", o, h), piece, piece, z_peer(o), s)
    for d in (2, 1, 3):
        send(("y", d), main, main, y_peer(d), s)

    for copy in loads:
        copy.wait()
    for t in range(COLS):
        columns = slice(t * LANES, (t + 1) * LANES)
        here = slice(t, t + 1)
        for c in range(3):
            for e in range(LOCAL):
                at = c * LOCAL + e
                for side, edge, step in ((0, ROWS - 1, -1), (1, 0, 1)):
                    second = edge + step
                    FE_out[side, at, here, :] = XN[c, e, edge : edge + 1, columns]
                    FE_out[side, 12 + at, here, :] = XN[c, e, second : second + 1, columns]
                    FE_out[side, 24 + at, here, :] = N[c, e, edge : edge + 1, columns]
        for side, edge in ((0, ROWS - 1), (1, 0)):
            FE_out[side, EDGE - 1, here, :] = G[edge : edge + 1, columns].astype(F32)
    send(("frow", 0), FE_out.at[0], FE_in.at[0], f, s_up)
    send(("frow", 1), FE_out.at[1], FE_in.at[1], f, s_down)

    for d in (0, 1):
        arrive(("vrow", d), VR_in.at[d])
    speed = M_own[...]
    for d in range(1, TILES):
        arrive(("max", d), M_all.at[d])
        speed = jnp.maximum(speed, M_all[d])
    speed = jnp.max(speed, axis=0, keepdims=True)
    above = jnp.where(first, 0.0, VR_in[0, 6:8, :])
    below = jnp.where(last, 0.0, VR_in[1, 0:2, :])
    PG[f, ROWS : ROWS + 2, :] = above
    PG[f, ROWS + 2 : ROWS + 4, :] = below
    PG[f, ROWS + 4 : PACKED, :] = jnp.broadcast_to(speed, (PACKED - ROWS - 4, LANES))
    rim = PG.at[f, ROWS:PACKED]
    for d in range(1, TILES):
        send(("rim", d), rim, rim, (f + d) % TILES, s)

    for h in range(CHUNKS):
        for o in (1, 3, 2):
            piece = PG.at[peer_back(o, 0), h * PIECE : (h + 1) * PIECE]
            arrive(("z", o, h), piece)
            for d in (2, 1, 3):
                send(("zy", o, d, h), piece, piece, y_peer(d), s)
    VC_out[0:8, :] = VR_in[0, 0:8, :]
    VC_out[8:16, :] = VR_in[1, 0:8, :]
    send(("vcorner", 0), VC_out, VC_in.at[0], f_up, s)
    send(("vcorner", 1), VC_out, VC_in.at[1], f_down, s)

    def block_at(t):
        return pl.ds(pl.multiple_of(t * LANES, LANES), LANES)

    def prepare(i, carry):
        t, r = i // 8, i % 8
        rows, rows_in = pl.ds(pl.multiple_of(r * 8, 8), 8), pl.ds(pl.multiple_of(r * 8 + HALO, 8), 8)
        here_at, before_at = block_at(t), block_at(jnp.maximum(t - 1, 0))
        after_at = block_at(jnp.minimum(t + 1, COLS - 1))
        for c in range(3):
            outside = float(c != 1)
            for e in range(LOCAL):
                here = XN[c, e, rows, here_at]
                before = jnp.where(t == 0, outside, XN[c, e, rows, before_at])
                after = jnp.where(t == COLS - 1, outside, XN[c, e, rows, after_at])
                XC[c, e, t, rows_in, :] = here
                XL[c, e, t, rows, :] = pltpu.roll(jnp.where(at_right, before, here), 1, axis=1)
                XR[c, e, t, rows, :] = pltpu.roll(jnp.where(at_left, after, here), LANES - 1, axis=1)
        return carry

    lax.fori_loop(0, 64, prepare, 0)
    for t in (0, COLS + 1):
        U[:, :, t * LANES : (t + 1) * LANES] = jnp.zeros((2, TALL, LANES), F32)
        S[:, t, :, :] = jnp.zeros((3, TALL, LANES), F32)
    for d in (0, 1):
        arrive(("frow", d), FE_in.at[d])
    for c in range(3):
        outside = float(c != 1)
        for e in range(LOCAL):
            row_above = jnp.where(first, outside, FE_in[0, c * LOCAL + e])
            row_below = jnp.where(last, outside, FE_in[1, c * LOCAL + e])
            for t in range(COLS):
                XC[c, e, t, HALO - 1 : HALO, :] = row_above[t : t + 1]
                XC[c, e, t, HALO + ROWS : HALO + ROWS + 1, :] = row_below[t : t + 1]

    for d in (1, 2, 3):
        arrive(("y", d), PG.at[peer_back(0, d), 0:ROWS])
    for o in (1, 3, 2):
        for d in (1, 2, 3):
            for h in range(CHUNKS):
                arrive(("zy", o, d, h), PG.at[peer_back(o, d), h * PIECE : (h + 1) * PIECE])
    for d in range(1, TILES):
        arrive(("rim", d), PG.at[(f + TILES - d) % TILES, ROWS:PACKED])

    low_tile = lax.broadcasted_iota(jnp.int32, (PACKED, LANES), 1) < TILE
    speed = jnp.zeros((1, LANES), F32)
    for t in range(COLS):
        even, odd = PG[2 * t], PG[2 * t + 1]
        u = jnp.where(low_tile, even, pltpu.roll(odd, TILE, axis=1))
        w = jnp.where(low_tile, pltpu.roll(even, TILE, axis=1), odd)
        columns = slice((t + 1) * LANES, (t + 2) * LANES)
        here = slice(t, t + 1)
        for c, strip in ((0, u), (1, w)):
            U[c, HALO : HALO + ROWS, columns] = strip[0:ROWS]
            U[c, HALO - 2 : HALO, columns] = strip[ROWS : ROWS + 2]
            U[c, HALO + ROWS : HALO + ROWS + 2, columns] = strip[ROWS + 2 : ROWS + 4]
            UE[0, c, 0, here, :] = strip[ROWS + 1 : ROWS + 2]
            UE[0, c, 1, here, :] = strip[ROWS : ROWS + 1]
            UE[0, c, 2, here, :] = strip[0:1]
            UE[1, c, 0, here, :] = strip[ROWS + 2 : ROWS + 3]
            UE[1, c, 1, here, :] = strip[ROWS - 1 : ROWS]
            UE[1, c, 2, here, :] = strip[ROWS + 3 : ROWS + 4]
        speed = jnp.maximum(speed, jnp.maximum(even[ROWS + 4 : ROWS + 5], odd[ROWS + 4 : ROWS + 5]))
    speed = jnp.max(speed, axis=1, keepdims=True)
    step = COURANT / (speed + SPEED_EPS)
    step = jnp.broadcast_to(step, (8, LANES))
    scale = jnp.sqrt(step / RELAX)

    def stress_of(total, weight):
        weight = MODULUS / FIELDS * weight
        return (
            weight * (total[0] - float(LOCAL)),
            weight * total[1],
            weight * (total[2] - float(LOCAL)),
        )

    def added(total, new):
        return new if total is None else tuple(a + b for a, b in zip(total, new))

    def spread(centre, above, below, outside):
        to_right = pltpu.roll(centre, 1, axis=1)
        to_left = pltpu.roll(centre, LANES - 1, axis=1)
        before = jnp.where(at_top, outside, pltpu.roll(to_right, 1, axis=0))
        after = jnp.where(at_bottom, outside, pltpu.roll(to_left, 7, axis=0))
        left = jnp.where(at_left, before, to_right)
        right = jnp.where(at_right, after, to_left)
        return centre, above, below, left, right

    for side, absent, place in ((0, first, HALO - 1), (1, last, HALO + ROWS)):
        weights = coefficients(step, *(spread(*(UE[side, c, q] for q in range(3)), 0.0) for c in range(2)))
        total = None
        for e in range(LOCAL):
            tensors = []
            for c in range(3):
                at = c * LOCAL + e
                centre, outer, inner = FE_in[side, at], FE_in[side, 12 + at], FE_out[1 - side, at]
                above, below = (outer, inner) if side == 0 else (inner, outer)
                tensors.append(spread(centre, above, below, float(c != 1)))
            noises = [FE_in[side, 24 + c * LOCAL + e] for c in range(3)]
            total = added(total, update(weights, scale, tensors, noises))
        for c, values in enumerate(stress_of(total, FE_in[side, EDGE - 1])):
            values = jnp.where(absent, 0.0, values)
            for t in range(COLS):
                S[c, t + 1, place : place + 1, :] = values[t : t + 1]

    def nearby(ref, lead, r, t):
        rows, columns = pl.ds(pl.multiple_of(r * 8 + HALO, 8), 8), block_at(t)
        rows_above = pl.ds(pl.multiple_of(r * 8, 8), 8)
        rows_below = pl.ds(pl.multiple_of(r * 8 + 2 * HALO, 8), 8)
        here = ref[(*lead, rows, columns)]
        above = jnp.where(at_bottom, ref[(*lead, rows_above, columns)], here)
        below = jnp.where(at_top, ref[(*lead, rows_below, columns)], here)
        left = jnp.where(at_right, ref[(*lead, rows, block_at(t - 1))], here)
        right = jnp.where(at_left, ref[(*lead, rows, block_at(t + 1))], here)
        return (
            here,
            pltpu.roll(above, 1, axis=0),
            pltpu.roll(below, 7, axis=0),
            pltpu.roll(left, 1, axis=1),
            pltpu.roll(right, LANES - 1, axis=1),
        )

    start = 2 * ((zh + 1) % RING) + COLS - 1

    def advance(i, carry):
        t = (start + i // 4) % COLS
        for part in (0, 1):
            r = i % 4 * 2 + part
            rows, columns = pl.ds(pl.multiple_of(r * 8, 8), 8), block_at(t)
            rows_in = pl.ds(pl.multiple_of(r * 8 + HALO, 8), 8)
            rows_above, rows_below = pl.ds(r * 8 + HALO - 1, 8), pl.ds(r * 8 + HALO + 1, 8)
            weights = coefficients(step, nearby(U, (0,), r, t + 1), nearby(U, (1,), r, t + 1))
            total = None
            for e in range(LOCAL):
                tensors = [
                    (
                        XC[c, e, t, rows_in, :],
                        XC[c, e, t, rows_above, :],
                        XC[c, e, t, rows_below, :],
                        XL[c, e, t, rows, :],
                        XR[c, e, t, rows, :],
                    )
                    for c in range(3)
                ]
                noises = [N[c, e, rows, columns] for c in range(3)]
                new = update(weights, scale, tensors, noises)
                for c in range(3):
                    N[c, e, rows, columns] = new[c]
                total = added(total, new)
            weight = G[rows, columns].astype(F32)
            for c, values in enumerate(stress_of(total, weight)):
                S[c, t + 1, rows_in, :] = values
        return carry

    def forces(j):
        block = (zh + 1 + j) % RING

        def body(tt, carry):
            t = 2 * block + tt + 1
            for r in range(ROWS // 8):
                top = r * 8 + HALO
                rows = slice(top, top + 8)

                def along_rows(c):
                    return S[c, t, top + 1 : top + 9, :] - S[c, t, top - 1 : top + 7, :]

                def along_cols(c):
                    here = S[c, t, rows, :]
                    left = jnp.where(at_right, S[c, t - 1, rows, :], here)
                    right = jnp.where(at_left, S[c, t + 1, rows, :], here)
                    return pltpu.roll(right, LANES - 1, axis=1) - pltpu.roll(left, 1, axis=1)

                down = 0.5 * (along_rows(0) + along_cols(1))
                across = 0.5 * (along_rows(1) + along_cols(2))
                packed = slice(r * 8, r * 8 + 8)
                Q[j, 2 * tt, packed, :] = jnp.where(low, down, pltpu.roll(across, TILE, axis=1))
                Q[j, 2 * tt + 1, packed, :] = jnp.where(low, pltpu.roll(down, TILE, axis=1), across)
            return carry

        lax.fori_loop(0, 2, body, 0)
        for d in (2, 1, 3):
            send(("part", j, d), Q.at[j, (y + d) % RING], Y_in.at[j, d - 1], y_peer(d), s)

    wide_lane = lax.broadcasted_iota(jnp.int32, (ROWS, LANES), 1)

    def edges(tile):
        turned = pltpu.roll(tile, HALO + TILE, axis=1)
        for wide in (
            jnp.where(wide_lane < 8, turned, pltpu.roll(tile, 16, axis=1)),
            jnp.where(wide_lane < 8, tile, turned),
        ):
            folded = wide[0:8]
            for block in range(1, 8):
                part = pltpu.roll(wide[8 * block : 8 * block + 8], 16 * block, axis=1)
                folded = jnp.where(lane >= 16 * block, part, folded)
            yield folded

    def ring_sum(j):
        owner = z_peer(j + 1)
        neighbours = (0, (owner + 1) % TILES), (1, (owner + TILES - 1) % TILES)
        for d in (1, 2, 3):
            arrive(("part", j, d), Y_in.at[j, d - 1])
        tile = (Q[j, y] + Y_in[j, 0]) + (Y_in[j, 1] + Y_in[j, 2])
        T[j] = tile
        ends = (0, s_up, T.at[j, ROWS - 8 : ROWS]), (1, s_down, T.at[j, 0:8])
        for b, to_s, rows in ends:
            for a, to_f in neighbours:
                send(("corner", a, b, j), rows, K_in.at[a, b, j], to_f, to_s)
        if j < 3:
            send(("sum", j), T.at[j], Z_in.at[j], owner, s)
        for b, to_s, rows in ends:
            send(("end", b, j), rows, E_in.at[b, j], owner, to_s)
        for (a, to_f), edge in zip(neighbours, edges(tile)):
            C[j, a] = edge
            send(("side", a, j), C.at[j, a], C_in.at[a, j], to_f, s)

    lax.fori_loop(0, 16, advance, 0)
    forces(0)
    lax.fori_loop(16, 24, advance, 0)
    forces(1)
    lax.fori_loop(24, 32, advance, 0)
    forces(2)
    forces(3)
    store = pltpu.make_async_copy(N, fields_out, local_sem.at[8])
    store.start()
    ring_sum(0)
    ring_sum(1)
    ring_sum(2)

    at_row = lax.broadcasted_iota(jnp.int32, (TALL, LANES), 0) + (s * ROWS - HALO)
    at_lane = lax.broadcasted_iota(jnp.int32, (TALL, LANES), 1)
    at_col = at_lane + (f * TILE - HALO)
    inside = (at_row >= 0) & (at_row < TILES * ROWS) & (at_col >= 0) & (at_col < TILES * TILE)
    inside = inside & (at_lane < TALL)
    for d in (0, 1):
        arrive(("vcorner", d), VC_in.at[d])

    near = lambda values: pltpu.roll(values, HALO, axis=1)
    far = lambda values: pltpu.roll(values, HALO + TILE, axis=1)

    def window(before, here, after):
        joined = jnp.where(at_lane < HALO, before, jnp.where(at_lane < HALO + TILE, here, after))
        return jnp.where(inside, joined, 0.0)

    def stacked(rim_rows, tile):
        return jnp.concatenate([rim_rows[0:8], PG[tile, 0:ROWS, :], rim_rows[8:16]], axis=0)

    v_before, v_here, v_after = (
        stacked(VC_in.at[0], f_down), stacked(VC_out, f), stacked(VC_in.at[1], f_up)
    )
    speeds = (
        window(far(v_before), near(v_here), far(v_after)),
        window(near(v_before), far(v_here), near(v_after)),
    )
    mask = jnp.concatenate([VR_in[0, 8:16, :], walls(slice(0, ROWS)), VR_in[1, 8:16, :]], axis=0)
    weight = BETA + 4.0 * VISCOSITY + PENALTY * (1.0 - mask)

    def apply(values):
        around = (
            pltpu.roll(values, TALL - 1, axis=0)
            + pltpu.roll(values, 1, axis=0)
            + pltpu.roll(values, LANES - 1, axis=1)
            + pltpu.roll(values, 1, axis=1)
        )
        return weight * values - VISCOSITY * around

    residual = [BETA * v - apply(v) for v in speeds]

    ring_sum(3)
    total = T[3]
    for j in range(3):
        arrive(("sum", j), Z_in.at[j])
        total = total + Z_in[j]
    for j in range(4):
        for b in (0, 1):
            for a in (0, 1):
                arrive(("corner", a, b, j), K_in.at[a, b, j])
            arrive(("end", b, j), E_in.at[b, j])
        for a in (0, 1):
            arrive(("side", a, j), C_in.at[a, j])

    def summed(ref, *lead):
        return (ref[(*lead, 0)] + ref[(*lead, 1)]) + (ref[(*lead, 2)] + ref[(*lead, 3)])

    def beside(a, turn, first, second):
        folded = summed(C_in, a)
        corners = [summed(K_in, a, b) for b in (0, 1)]
        return tuple(
            jnp.concatenate(
                [place(corners[0])]
                + [pltpu.roll(folded, (turn - 16 * block - 8 * c) % LANES, axis=1) for block in range(8)]
                + [place(corners[1])],
                axis=0,
            )
            for c, place in enumerate((first, second))
        )

    f_before = beside(0, 0, far, near)
    f_after = beside(1, HALO + TILE, far, near)
    f_here = jnp.concatenate([summed(E_in, 0), total, summed(E_in, 1)], axis=0)
    force = (
        window(f_before[0], near(f_here), f_after[0]),
        window(f_before[1], far(f_here), f_after[1]),
    )

    centre = 0.5 * (UPPER + LOWER)
    radius = 0.5 * (UPPER - LOWER)
    sigma = centre / radius
    for c in range(2):
        rho = 1.0 / sigma
        v = speeds[c]
        r = jnp.where(inside, residual[c] + force[c], 0.0)
        d = r / centre
        for index in range(ITERS):
            v = v + d
            if index + 1 < ITERS:
                r = jnp.where(inside, r - apply(d), 0.0)
                rho_next = 1.0 / (2.0 * sigma - rho)
                d = rho_next * rho * d + 2.0 * rho_next / radius * r
                rho = rho_next
        velocity_out[c, :, :] = pltpu.roll(v, LANES - HALO, axis=1)[HALO : HALO + ROWS, 0:TILE]

    for copy in started:
        copy.wait_send()
    store.wait()


def per_device(fields, increments, velocity, geometry):
    hbm = pl.BlockSpec(memory_space=pltpu.HBM)

    def vmem(*shape):
        return pltpu.VMEM(shape, F32)

    return pl.pallas_call(
        kernel,
        out_shape=(
            jax.ShapeDtypeStruct(fields.shape, F32),
            jax.ShapeDtypeStruct(velocity.shape, F32),
        ),
        in_specs=[hbm] * 4,
        out_specs=(hbm, pl.BlockSpec(memory_space=pltpu.VMEM)),
        scratch_shapes=[
            vmem(3, LOCAL, ROWS, COLS * LANES),
            vmem(3, LOCAL, COLS, TALL, LANES),
            vmem(3, LOCAL, COLS, ROWS, LANES),
            vmem(3, LOCAL, COLS, ROWS, LANES),
            vmem(3, LOCAL, ROWS, COLS * LANES),
            vmem(2, ROWS, TILE),
            pltpu.VMEM((ROWS, COLS * LANES), jnp.int32),
            vmem(2, TALL, (COLS + 2) * LANES),
            vmem(2, 2, 3, COLS, LANES),
            vmem(3, COLS + 2, TALL, LANES),
            vmem(TILES, PACKED, LANES),
            vmem(8, LANES),
            vmem(TILES, 8, LANES),
            vmem(2, 16, LANES),
            vmem(2, 16, LANES),
            vmem(2, EDGE, COLS, LANES),
            vmem(2, EDGE, COLS, LANES),
            vmem(16, LANES),
            vmem(2, 16, LANES),
            vmem(RING, RING, ROWS, LANES),
            vmem(RING, 3, ROWS, LANES),
            vmem(3, ROWS, LANES),
            vmem(RING, ROWS, LANES),
            vmem(RING, 2, 8, LANES),
            vmem(2, RING, 8, LANES),
            vmem(2, RING, 8, LANES),
            vmem(2, 2, RING, 8, LANES),
            pltpu.SemaphoreType.DMA((9,)),
            pltpu.SemaphoreType.DMA((len(SLOTS),)),
            pltpu.SemaphoreType.DMA((len(SLOTS),)),
        ],
        compiler_params=pltpu.CompilerParams(
            collective_id=0, has_side_effects=True, vmem_limit_bytes=VMEM_LIMIT
        ),
        name="step",
    )(fields, increments, velocity, geometry)


def solution(mesh):
    placed = (
        P(None, "field", "space", None),
        P(None, "field", "space", None),
        P(None, "space", "field"),
        P("space", None),
    )
    return jax.shard_map(
        per_device,
        mesh=mesh,
        in_specs=placed,
        out_specs=(P(None, "field", "space", None), P(None, "space", "field")),
        check_vma=False,
    )
```

```python
import functools

import jax
import jax.numpy as jnp
from jax import lax
from jax.experimental import pallas as pl
from jax.experimental.pallas import tpu as pltpu
from jax.sharding import PartitionSpec as P

ITERS = 8
COURANT = 0.5
SPEED_EPS = 1e-06
RELAX = 0.5
MODULUS = 2.0
BETA = 0.5
VISCOSITY = 1.0
PENALTY = 20.0
LOWER = BETA
UPPER = BETA + PENALTY + 8.0 * VISCOSITY

MESH = pl.DeviceIdType.MESH
F32 = jnp.float32
LANES = 128
ROWS = 64
HALO = 8
TALL = ROWS + 2 * HALO
TILE = 64
TILES = 16
COLS = 8
FIELDS = 64
LOCAL = 4
VMEM_LIMIT = 63 * 1024 * 1024
RING = 4
CHUNKS = 2
PIECE = ROWS // CHUNKS
PACKED = 72
EDGE = 12 * 3 + 1


def slots():
    names = [(n, d) for n in ("max",) for d in range(1, 16)]
    names += [("rim", o, d) for o in range(4) for d in range(4) if o or d]
    names += [(n, d) for n in ("vrow", "frow", "vcorner") for d in (0, 1)]
    names += [("y", d) for d in (1, 2, 3)]
    names += [("z", o, h) for o in (1, 2, 3) for h in range(CHUNKS)]
    names += [("zy", o, d, h) for o in (1, 2, 3) for d in (1, 2, 3) for h in range(CHUNKS)]
    names += [("part", j, d) for j in range(4) for d in (1, 2, 3)]
    names += [("sum", j) for j in range(3)]
    names += [(n, d, j) for n in ("side", "end") for d in (0, 1) for j in range(4)]
    names += [("corner", a, b, j) for a in (0, 1) for b in (0, 1) for j in range(4)]
    return {name: at for at, name in enumerate(names)}


SLOTS = slots()


def coefficients(step, u, w):
    (u, u_above, u_below, u_left, u_right), (w, w_above, w_below, w_left, w_right) = u, w
    half_step = 0.5 * step
    down_down = half_step * (u_below - u_above)
    down_across = half_step * (u_right - u_left)
    across_down = half_step * (w_below - w_above)
    across_across = half_step * (w_right - w_left)
    down, across = step * jnp.abs(u), step * jnp.abs(w)
    relaxed = step * (1.0 / RELAX)
    kept = 1.0 - relaxed - down - across
    own = (
        kept + 2.0 * down_down,
        kept + (down_down + across_across),
        kept + 2.0 * across_across,
    )
    return own, (u > 0.0, w > 0.0), (down, across), down_across, across_down, relaxed


def update(weights, scale, tensors, noises):
    own, (downward, rightward), (down, across), down_across, across_down, relaxed = weights
    new = []
    for c in range(3):
        here, above, below, left, right = tensors[c]
        upwind = down * jnp.where(downward, above, below)
        sidewind = across * jnp.where(rightward, left, right)
        new.append((own[c] * here + scale * noises[c]) + (upwind + sidewind))
    xx, xy, yy = (tensor[0] for tensor in tensors)
    return (
        new[0] + (2.0 * down_across * xy + relaxed),
        new[1] + (down_across * yy + across_down * xx),
        new[2] + (2.0 * across_down * xy + relaxed),
    )


def kernel(
    fields, noise, velocity, geometry, fields_out, velocity_out,
    XN, XC, XL, XR, N, V, G, U, UE, S, PG, M_own, M_all, VR_out, VR_in, FE_out, FE_in, VC_out, VC_in,
    Q, Y_in, Z_in, T, C, C_in, E_in, K_in, local_sem, send_sem, recv_sem,
):
    f = lax.axis_index("field")
    s = lax.axis_index("space")
    zh = f // RING
    y = f % RING
    f_up, f_down = (f + 1) % TILES, (f + TILES - 1) % TILES
    s_up, s_down = (s + 1) % TILES, (s + TILES - 1) % TILES
    first, last = s == 0, s == TILES - 1

    def y_peer(d):
        return zh * RING + (y + d) % RING

    def z_peer(o):
        return (zh + o) % RING * RING + y

    def peer_back(o, d):
        return (zh + RING - o) % RING * RING + (y + RING - d) % RING

    started = []

    def send(name, source, target, to_f, to_s):
        copy = pltpu.make_async_remote_copy(
            src_ref=source,
            dst_ref=target,
            send_sem=send_sem.at[SLOTS[name]],
            recv_sem=recv_sem.at[SLOTS[name]],
            device_id=(to_f, to_s),
            device_id_type=MESH,
        )
        copy.start()
        started.append(copy)

    def arrive(name, landed):
        pltpu.make_async_copy(landed, landed, recv_sem.at[SLOTS[name]]).wait()

    barrier = pltpu.get_barrier_semaphore()
    partners = [(f, (s + d) % TILES) for d in range(1, TILES)]
    partners += [(y_peer(d), s) for d in (1, 2, 3)] + [(z_peer(d), s) for d in (1, 2, 3)]
    for partner in partners:
        pl.semaphore_signal(barrier, inc=1, device_id=partner, device_id_type=MESH)

    load_v = pltpu.make_async_copy(velocity, V, local_sem.at[0])
    load_v.start()
    load_g = pltpu.make_async_copy(geometry, G, local_sem.at[1])
    load_g.start()
    loads = []
    for c in range(3):
        loads.append(pltpu.make_async_copy(fields.at[c], XN.at[c], local_sem.at[2 + c]))
    for c in range(3):
        loads.append(pltpu.make_async_copy(noise.at[c], N.at[c], local_sem.at[5 + c]))
    for copy in loads:
        copy.start()

    lane = lax.broadcasted_iota(jnp.int32, (8, LANES), 1)
    row = lax.broadcasted_iota(jnp.int32, (8, LANES), 0)
    low = lane < TILE
    at_left, at_right = lane == 0, lane == LANES - 1
    at_top, at_bottom = row == 0, row == 7

    load_v.wait()
    own = jnp.concatenate([V[0], V[1]], axis=1)
    PG[f, 0:ROWS, :] = own
    M_own[...] = jnp.max(jnp.abs(own).reshape(ROWS // 8, 8, LANES), axis=0)
    VR_out[0, 0:8, :] = own[ROWS - 8 :]
    VR_out[1, 0:8, :] = own[0:8]

    load_g.wait()
    half = f % 2
    t_own = f // 2

    def walls(rows):
        def block(t):
            at = pl.multiple_of(jnp.clip(t, 0, COLS - 1) * LANES, LANES)
            return G[rows, pl.ds(at, LANES)].astype(F32)

        before, here, after = block(t_own - 1), block(t_own), block(t_own + 1)
        count = here.shape[0]
        at = lax.broadcasted_iota(jnp.int32, (count, LANES), 1)
        even = pltpu.roll(jnp.where(at < 120, here, before), HALO, axis=1)
        odd = pltpu.roll(jnp.where(at < HALO, after, here), HALO + TILE, axis=1)
        return jnp.where(half == 0, even, odd)

    VR_out[0, 8:16, :] = walls(slice(ROWS - 8, ROWS))
    VR_out[1, 8:16, :] = walls(slice(0, 8))

    pl.semaphore_wait(barrier, len(partners))

    send(("vrow", 0), VR_out.at[0], VR_in.at[0], f, s_up)
    send(("vrow", 1), VR_out.at[1], VR_in.at[1], f, s_down)
    for d in range(1, TILES):
        send(("max", d), M_own, M_all.at[d], f, (s + d) % TILES)
    main = PG.at[f, 0:ROWS]
    for h in range(CHUNKS):
        piece = PG.at[f, h * PIECE : (h + 1) * PIECE]
        for o in (2, 1, 3):
            send(("z", o, h), piece, piece, z_peer(o), s)
    for d in (2, 1, 3):
        send(("y", d), main, main, y_peer(d), s)

    for copy in loads:
        copy.wait()
    for t in range(COLS):
        columns = slice(t * LANES, (t + 1) * LANES)
        here = slice(t, t + 1)
        for c in range(3):
            for e in range(LOCAL):
                at = c * LOCAL + e
                for side, edge, step in ((0, ROWS - 1, -1), (1, 0, 1)):
                    second = edge + step
                    FE_out[side, at, here, :] = XN[c, e, edge : edge + 1, columns]
                    FE_out[side, 12 + at, here, :] = XN[c, e, second : second + 1, columns]
                    FE_out[side, 24 + at, here, :] = N[c, e, edge : edge + 1, columns]
        for side, edge in ((0, ROWS - 1), (1, 0)):
            FE_out[side, EDGE - 1, here, :] = G[edge : edge + 1, columns].astype(F32)
    send(("frow", 0), FE_out.at[0], FE_in.at[0], f, s_up)
    send(("frow", 1), FE_out.at[1], FE_in.at[1], f, s_down)

    for d in (0, 1):
        arrive(("vrow", d), VR_in.at[d])
    speed = M_own[...]
    for d in range(1, TILES):
        arrive(("max", d), M_all.at[d])
        speed = jnp.maximum(speed, M_all[d])
    speed = jnp.max(speed, axis=0, keepdims=True)
    above = jnp.where(first, 0.0, VR_in[0, 6:8, :])
    below = jnp.where(last, 0.0, VR_in[1, 0:2, :])
    PG[f, ROWS : ROWS + 2, :] = above
    PG[f, ROWS + 2 : ROWS + 4, :] = below
    PG[f, ROWS + 4 : PACKED, :] = jnp.broadcast_to(speed, (PACKED - ROWS - 4, LANES))
    rim = PG.at[f, ROWS:PACKED]

    def send_rim(o, d):
        send(("rim", o, d), rim, rim, (zh + o) % RING * RING + (y + d) % RING, s)

    for at in (1, 2, 3):
        send_rim(at, 0)
        send_rim(0, at)

    for h in range(CHUNKS):
        for o in (1, 3, 2):
            piece = PG.at[peer_back(o, 0), h * PIECE : (h + 1) * PIECE]
            arrive(("z", o, h), piece)
            for d in (2, 1, 3):
                send(("zy", o, d, h), piece, piece, y_peer(d), s)
            if h == 0:
                for d in (2, 1, 3):
                    send_rim(RING - o, d)
    VC_out[0:8, :] = VR_in[0, 0:8, :]
    VC_out[8:16, :] = VR_in[1, 0:8, :]
    send(("vcorner", 0), VC_out, VC_in.at[0], f_up, s)
    send(("vcorner", 1), VC_out, VC_in.at[1], f_down, s)

    def block_at(t):
        return pl.ds(pl.multiple_of(t * LANES, LANES), LANES)

    def prepare(i, carry):
        t, r = i // 8, i % 8
        rows, rows_in = pl.ds(pl.multiple_of(r * 8, 8), 8), pl.ds(pl.multiple_of(r * 8 + HALO, 8), 8)
        here_at, before_at = block_at(t), block_at(jnp.maximum(t - 1, 0))
        after_at = block_at(jnp.minimum(t + 1, COLS - 1))
        for c in range(3):
            outside = float(c != 1)
            for e in range(LOCAL):
                here = XN[c, e, rows, here_at]
                before = jnp.where(t == 0, outside, XN[c, e, rows, before_at])
                after = jnp.where(t == COLS - 1, outside, XN[c, e, rows, after_at])
                XC[c, e, t, rows_in, :] = here
                XL[c, e, t, rows, :] = pltpu.roll(jnp.where(at_right, before, here), 1, axis=1)
                XR[c, e, t, rows, :] = pltpu.roll(jnp.where(at_left, after, here), LANES - 1, axis=1)
        return carry

    lax.fori_loop(0, 64, prepare, 0)
    for t in (0, COLS + 1):
        U[:, :, t * LANES : (t + 1) * LANES] = jnp.zeros((2, TALL, LANES), F32)
        S[:, t, :, :] = jnp.zeros((3, TALL, LANES), F32)
    for d in (0, 1):
        arrive(("frow", d), FE_in.at[d])
    for c in range(3):
        outside = float(c != 1)
        for e in range(LOCAL):
            row_above = jnp.where(first, outside, FE_in[0, c * LOCAL + e])
            row_below = jnp.where(last, outside, FE_in[1, c * LOCAL + e])
            for t in range(COLS):
                XC[c, e, t, HALO - 1 : HALO, :] = row_above[t : t + 1]
                XC[c, e, t, HALO + ROWS : HALO + ROWS + 1, :] = row_below[t : t + 1]

    low_tile = lax.broadcasted_iota(jnp.int32, (PACKED, LANES), 1) < TILE
    speed = jnp.zeros((1, LANES), F32)
    for o in range(4):
        for d in range(4):
            if o or d:
                arrive(("rim", o, d), PG.at[peer_back(o, d), ROWS:PACKED])
    for o in (0, 1, 3, 2):
        for d in (1, 2, 3):
            if o == 0:
                arrive(("y", d), PG.at[peer_back(0, d), 0:ROWS])
            else:
                for h in range(CHUNKS):
                    arrive(("zy", o, d, h), PG.at[peer_back(o, d), h * PIECE : (h + 1) * PIECE])
        for tt in (0, 1):
            t = (zh + RING - o) % RING * 2 + tt
            even, odd = PG[2 * t], PG[2 * t + 1]
            u = jnp.where(low_tile, even, pltpu.roll(odd, TILE, axis=1))
            w = jnp.where(low_tile, pltpu.roll(even, TILE, axis=1), odd)
            columns = block_at(t + 1)
            for c, strip in ((0, u), (1, w)):
                U[c, HALO : HALO + ROWS, columns] = strip[0:ROWS]
                U[c, HALO - 2 : HALO, columns] = strip[ROWS : ROWS + 2]
                U[c, HALO + ROWS : HALO + ROWS + 2, columns] = strip[ROWS + 2 : ROWS + 4]
            speed = jnp.maximum(
                speed, jnp.maximum(even[ROWS + 4 : ROWS + 5], odd[ROWS + 4 : ROWS + 5])
            )
    for t in range(COLS):
        columns = slice((t + 1) * LANES, (t + 2) * LANES)
        here = slice(t, t + 1)
        for c in range(2):
            for side, rows in ((0, (HALO - 1, HALO - 2, HALO)), (1, (HALO + ROWS, HALO + ROWS - 1, HALO + ROWS + 1))):
                for q, at in enumerate(rows):
                    UE[side, c, q, here, :] = U[c, at : at + 1, columns]
    speed = jnp.max(speed, axis=1, keepdims=True)
    step = COURANT / (speed + SPEED_EPS)
    step = jnp.broadcast_to(step, (8, LANES))
    scale = jnp.sqrt(step / RELAX)

    def stress_of(total, weight):
        weight = MODULUS / FIELDS * weight
        return (
            weight * (total[0] - float(LOCAL)),
            weight * total[1],
            weight * (total[2] - float(LOCAL)),
        )

    def added(total, new):
        return new if total is None else tuple(a + b for a, b in zip(total, new))

    def spread(centre, above, below, outside):
        to_right = pltpu.roll(centre, 1, axis=1)
        to_left = pltpu.roll(centre, LANES - 1, axis=1)
        before = jnp.where(at_top, outside, pltpu.roll(to_right, 1, axis=0))
        after = jnp.where(at_bottom, outside, pltpu.roll(to_left, 7, axis=0))
        left = jnp.where(at_left, before, to_right)
        right = jnp.where(at_right, after, to_left)
        return centre, above, below, left, right

    for side, absent, place in ((0, first, HALO - 1), (1, last, HALO + ROWS)):
        weights = coefficients(step, *(spread(*(UE[side, c, q] for q in range(3)), 0.0) for c in range(2)))
        total = None
        for e in range(LOCAL):
            tensors = []
            for c in range(3):
                at = c * LOCAL + e
                centre, outer, inner = FE_in[side, at], FE_in[side, 12 + at], FE_out[1 - side, at]
                above, below = (outer, inner) if side == 0 else (inner, outer)
                tensors.append(spread(centre, above, below, float(c != 1)))
            noises = [FE_in[side, 24 + c * LOCAL + e] for c in range(3)]
            total = added(total, update(weights, scale, tensors, noises))
        for c, values in enumerate(stress_of(total, FE_in[side, EDGE - 1])):
            values = jnp.where(absent, 0.0, values)
            for t in range(COLS):
                S[c, t + 1, place : place + 1, :] = values[t : t + 1]

    def nearby(ref, lead, r, t):
        rows, columns = pl.ds(pl.multiple_of(r * 8 + HALO, 8), 8), block_at(t)
        rows_above = pl.ds(pl.multiple_of(r * 8, 8), 8)
        rows_below = pl.ds(pl.multiple_of(r * 8 + 2 * HALO, 8), 8)
        here = ref[(*lead, rows, columns)]
        above = jnp.where(at_bottom, ref[(*lead, rows_above, columns)], here)
        below = jnp.where(at_top, ref[(*lead, rows_below, columns)], here)
        left = jnp.where(at_right, ref[(*lead, rows, block_at(t - 1))], here)
        right = jnp.where(at_left, ref[(*lead, rows, block_at(t + 1))], here)
        return (
            here,
            pltpu.roll(above, 1, axis=0),
            pltpu.roll(below, 7, axis=0),
            pltpu.roll(left, 1, axis=1),
            pltpu.roll(right, LANES - 1, axis=1),
        )

    start = 2 * ((zh + 1) % RING) + COLS - 1

    def advance(i, carry):
        t = (start + i // 4) % COLS
        for part in (0, 1):
            r = i % 4 * 2 + part
            rows, columns = pl.ds(pl.multiple_of(r * 8, 8), 8), block_at(t)
            rows_in = pl.ds(pl.multiple_of(r * 8 + HALO, 8), 8)
            rows_above, rows_below = pl.ds(r * 8 + HALO - 1, 8), pl.ds(r * 8 + HALO + 1, 8)
            weights = coefficients(step, nearby(U, (0,), r, t + 1), nearby(U, (1,), r, t + 1))
            total = None
            for e in range(LOCAL):
                tensors = [
                    (
                        XC[c, e, t, rows_in, :],
                        XC[c, e, t, rows_above, :],
                        XC[c, e, t, rows_below, :],
                        XL[c, e, t, rows, :],
                        XR[c, e, t, rows, :],
                    )
                    for c in range(3)
                ]
                noises = [N[c, e, rows, columns] for c in range(3)]
                new = update(weights, scale, tensors, noises)
                for c in range(3):
                    N[c, e, rows, columns] = new[c]
                total = added(total, new)
            weight = G[rows, columns].astype(F32)
            for c, values in enumerate(stress_of(total, weight)):
                S[c, t + 1, rows_in, :] = values
        return carry

    def forces(j):
        block = (zh + 1 + j) % RING

        def body(tt, carry):
            t = 2 * block + tt + 1
            for r in range(ROWS // 8):
                top = r * 8 + HALO
                rows = slice(top, top + 8)

                def along_rows(c):
                    return S[c, t, top + 1 : top + 9, :] - S[c, t, top - 1 : top + 7, :]

                def along_cols(c):
                    here = S[c, t, rows, :]
                    left = jnp.where(at_right, S[c, t - 1, rows, :], here)
                    right = jnp.where(at_left, S[c, t + 1, rows, :], here)
                    return pltpu.roll(right, LANES - 1, axis=1) - pltpu.roll(left, 1, axis=1)

                down = 0.5 * (along_rows(0) + along_cols(1))
                across = 0.5 * (along_rows(1) + along_cols(2))
                packed = slice(r * 8, r * 8 + 8)
                Q[j, 2 * tt, packed, :] = jnp.where(low, down, pltpu.roll(across, TILE, axis=1))
                Q[j, 2 * tt + 1, packed, :] = jnp.where(low, pltpu.roll(down, TILE, axis=1), across)
            return carry

        lax.fori_loop(0, 2, body, 0)
        for d in (2, 1, 3):
            send(("part", j, d), Q.at[j, (y + d) % RING], Y_in.at[j, d - 1], y_peer(d), s)

    wide_lane = lax.broadcasted_iota(jnp.int32, (ROWS, LANES), 1)

    def edges(tile):
        turned = pltpu.roll(tile, HALO + TILE, axis=1)
        for wide in (
            jnp.where(wide_lane < 8, turned, pltpu.roll(tile, 16, axis=1)),
            jnp.where(wide_lane < 8, tile, turned),
        ):
            folded = wide[0:8]
            for block in range(1, 8):
                part = pltpu.roll(wide[8 * block : 8 * block + 8], 16 * block, axis=1)
                folded = jnp.where(lane >= 16 * block, part, folded)
            yield folded

    def ring_sum(j):
        owner = z_peer(j + 1)
        neighbours = (0, (owner + 1) % TILES), (1, (owner + TILES - 1) % TILES)
        for d in (1, 2, 3):
            arrive(("part", j, d), Y_in.at[j, d - 1])
        tile = (Q[j, y] + Y_in[j, 0]) + (Y_in[j, 1] + Y_in[j, 2])
        T[j] = tile
        ends = (0, s_up, T.at[j, ROWS - 8 : ROWS]), (1, s_down, T.at[j, 0:8])
        for b, to_s, rows in ends:
            for a, to_f in neighbours:
                send(("corner", a, b, j), rows, K_in.at[a, b, j], to_f, to_s)
        if j < 3:
            send(("sum", j), T.at[j], Z_in.at[j], owner, s)
        for b, to_s, rows in ends:
            send(("end", b, j), rows, E_in.at[b, j], owner, to_s)
        for (a, to_f), edge in zip(neighbours, edges(tile)):
            C[j, a] = edge
            send(("side", a, j), C.at[j, a], C_in.at[a, j], to_f, s)

    lax.fori_loop(0, 16, advance, 0)
    forces(0)
    lax.fori_loop(16, 24, advance, 0)
    forces(1)
    lax.fori_loop(24, 32, advance, 0)
    forces(2)
    forces(3)
    store = pltpu.make_async_copy(N, fields_out, local_sem.at[8])
    store.start()
    at_row = lax.broadcasted_iota(jnp.int32, (TALL, LANES), 0) + (s * ROWS - HALO)
    at_lane = lax.broadcasted_iota(jnp.int32, (TALL, LANES), 1)
    at_col = at_lane + (f * TILE - HALO)
    inside = (at_row >= 0) & (at_row < TILES * ROWS) & (at_col >= 0) & (at_col < TILES * TILE)
    inside = inside & (at_lane < TALL)
    for d in (0, 1):
        arrive(("vcorner", d), VC_in.at[d])

    near = lambda values: pltpu.roll(values, HALO, axis=1)
    far = lambda values: pltpu.roll(values, HALO + TILE, axis=1)

    def window(before, here, after):
        joined = jnp.where(at_lane < HALO, before, jnp.where(at_lane < HALO + TILE, here, after))
        return jnp.where(inside, joined, 0.0)

    def stacked(rim_rows, tile):
        return jnp.concatenate([rim_rows[0:8], PG[tile, 0:ROWS, :], rim_rows[8:16]], axis=0)

    v_before, v_here, v_after = (
        stacked(VC_in.at[0], f_down), stacked(VC_out, f), stacked(VC_in.at[1], f_up)
    )
    speeds = (
        window(far(v_before), near(v_here), far(v_after)),
        window(near(v_before), far(v_here), near(v_after)),
    )
    mask = jnp.concatenate([VR_in[0, 8:16, :], walls(slice(0, ROWS)), VR_in[1, 8:16, :]], axis=0)
    weight = BETA + 4.0 * VISCOSITY + PENALTY * (1.0 - mask)

    def apply(values):
        around = (
            pltpu.roll(values, TALL - 1, axis=0)
            + pltpu.roll(values, 1, axis=0)
            + pltpu.roll(values, LANES - 1, axis=1)
            + pltpu.roll(values, 1, axis=1)
        )
        return weight * values - VISCOSITY * around

    residual = [BETA * v - apply(v) for v in speeds]

    ring_sum(0)
    ring_sum(1)
    ring_sum(2)
    ring_sum(3)
    total = T[3]
    for j in range(3):
        arrive(("sum", j), Z_in.at[j])
        total = total + Z_in[j]
    for j in range(4):
        for b in (0, 1):
            for a in (0, 1):
                arrive(("corner", a, b, j), K_in.at[a, b, j])
            arrive(("end", b, j), E_in.at[b, j])
        for a in (0, 1):
            arrive(("side", a, j), C_in.at[a, j])

    def summed(ref, *lead):
        return (ref[(*lead, 0)] + ref[(*lead, 1)]) + (ref[(*lead, 2)] + ref[(*lead, 3)])

    def beside(a, turn, first, second):
        folded = summed(C_in, a)
        corners = [summed(K_in, a, b) for b in (0, 1)]
        return tuple(
            jnp.concatenate(
                [place(corners[0])]
                + [pltpu.roll(folded, (turn - 16 * block - 8 * c) % LANES, axis=1) for block in range(8)]
                + [place(corners[1])],
                axis=0,
            )
            for c, place in enumerate((first, second))
        )

    f_before = beside(0, 0, far, near)
    f_after = beside(1, HALO + TILE, far, near)
    f_here = jnp.concatenate([summed(E_in, 0), total, summed(E_in, 1)], axis=0)
    force = (
        window(f_before[0], near(f_here), f_after[0]),
        window(f_before[1], far(f_here), f_after[1]),
    )

    centre = 0.5 * (UPPER + LOWER)
    radius = 0.5 * (UPPER - LOWER)
    sigma = centre / radius
    for c in range(2):
        rho = 1.0 / sigma
        v = speeds[c]
        r = jnp.where(inside, residual[c] + force[c], 0.0)
        d = r / centre
        for index in range(ITERS):
            v = v + d
            if index + 1 < ITERS:
                r = jnp.where(inside, r - apply(d), 0.0)
                rho_next = 1.0 / (2.0 * sigma - rho)
                d = rho_next * rho * d + 2.0 * rho_next / radius * r
                rho = rho_next
        velocity_out[c, :, :] = pltpu.roll(v, LANES - HALO, axis=1)[HALO : HALO + ROWS, 0:TILE]

    for copy in started:
        copy.wait_send()
    store.wait()


def per_device(fields, increments, velocity, geometry):
    hbm = pl.BlockSpec(memory_space=pltpu.HBM)

    def vmem(*shape):
        return pltpu.VMEM(shape, F32)

    return pl.pallas_call(
        kernel,
        out_shape=(
            jax.ShapeDtypeStruct(fields.shape, F32),
            jax.ShapeDtypeStruct(velocity.shape, F32),
        ),
        in_specs=[hbm] * 4,
        out_specs=(hbm, pl.BlockSpec(memory_space=pltpu.VMEM)),
        scratch_shapes=[
            vmem(3, LOCAL, ROWS, COLS * LANES),
            vmem(3, LOCAL, COLS, TALL, LANES),
            vmem(3, LOCAL, COLS, ROWS, LANES),
            vmem(3, LOCAL, COLS, ROWS, LANES),
            vmem(3, LOCAL, ROWS, COLS * LANES),
            vmem(2, ROWS, TILE),
            pltpu.VMEM((ROWS, COLS * LANES), jnp.int32),
            vmem(2, TALL, (COLS + 2) * LANES),
            vmem(2, 2, 3, COLS, LANES),
            vmem(3, COLS + 2, TALL, LANES),
            vmem(TILES, PACKED, LANES),
            vmem(8, LANES),
            vmem(TILES, 8, LANES),
            vmem(2, 16, LANES),
            vmem(2, 16, LANES),
            vmem(2, EDGE, COLS, LANES),
            vmem(2, EDGE, COLS, LANES),
            vmem(16, LANES),
            vmem(2, 16, LANES),
            vmem(RING, RING, ROWS, LANES),
            vmem(RING, 3, ROWS, LANES),
            vmem(3, ROWS, LANES),
            vmem(RING, ROWS, LANES),
            vmem(RING, 2, 8, LANES),
            vmem(2, RING, 8, LANES),
            vmem(2, RING, 8, LANES),
            vmem(2, 2, RING, 8, LANES),
            pltpu.SemaphoreType.DMA((9,)),
            pltpu.SemaphoreType.DMA((len(SLOTS),)),
            pltpu.SemaphoreType.DMA((len(SLOTS),)),
        ],
        compiler_params=pltpu.CompilerParams(
            collective_id=0, has_side_effects=True, vmem_limit_bytes=VMEM_LIMIT
        ),
        name="step",
    )(fields, increments, velocity, geometry)


def solution(mesh):
    placed = (
        P(None, "field", "space", None),
        P(None, "field", "space", None),
        P(None, "space", "field"),
        P("space", None),
    )
    return jax.shard_map(
        per_device,
        mesh=mesh,
        in_specs=placed,
        out_specs=(P(None, "field", "space", None), P(None, "space", "field")),
        check_vma=False,
    )
```

```python
import functools

import jax
import jax.numpy as jnp
from jax import lax
from jax.experimental import pallas as pl
from jax.experimental.pallas import tpu as pltpu
from jax.sharding import PartitionSpec as P

ITERS = 8
COURANT = 0.5
SPEED_EPS = 1e-06
RELAX = 0.5
MODULUS = 2.0
BETA = 0.5
VISCOSITY = 1.0
PENALTY = 20.0
LOWER = BETA
UPPER = BETA + PENALTY + 8.0 * VISCOSITY

MESH = pl.DeviceIdType.MESH
F32 = jnp.float32
LANES = 128
ROWS = 64
HALO = 8
TALL = ROWS + 2 * HALO
TILE = 64
TILES = 16
COLS = 8
FIELDS = 64
LOCAL = 4
VMEM_LIMIT = 63 * 1024 * 1024
RING = 4
CHUNKS = 1
PIECE = ROWS // CHUNKS
PACKED = 72
EDGE = 12 * 3 + 1


def slots():
    names = [(n, d) for n in ("max",) for d in range(1, 16)]
    names += [("rim", o, d) for o in range(4) for d in range(4) if o or d]
    names += [(n, d) for n in ("vrow", "frow", "vcorner") for d in (0, 1)]
    names += [("y", d) for d in (1, 2, 3)]
    names += [("z", o, h) for o in (1, 2, 3) for h in range(CHUNKS)]
    names += [("zy", o, d, h) for o in (1, 2, 3) for d in (1, 2, 3) for h in range(CHUNKS)]
    names += [("part", j, d) for j in range(4) for d in (1, 2, 3)]
    names += [("sum", j) for j in range(3)]
    names += [(n, d, j) for n in ("side", "end") for d in (0, 1) for j in range(4)]
    names += [("corner", a, b, j) for a in (0, 1) for b in (0, 1) for j in range(4)]
    return {name: at for at, name in enumerate(names)}


SLOTS = slots()


def coefficients(step, u, w):
    (u, u_above, u_below, u_left, u_right), (w, w_above, w_below, w_left, w_right) = u, w
    half_step = 0.5 * step
    down_down = half_step * (u_below - u_above)
    down_across = half_step * (u_right - u_left)
    across_down = half_step * (w_below - w_above)
    across_across = half_step * (w_right - w_left)
    down, across = step * jnp.abs(u), step * jnp.abs(w)
    relaxed = step * (1.0 / RELAX)
    kept = 1.0 - relaxed - down - across
    own = (
        kept + 2.0 * down_down,
        kept + (down_down + across_across),
        kept + 2.0 * across_across,
    )
    return own, (u > 0.0, w > 0.0), (down, across), down_across, across_down, relaxed


def update(weights, scale, tensors, noises):
    own, (downward, rightward), (down, across), down_across, across_down, relaxed = weights
    new = []
    for c in range(3):
        here, above, below, left, right = tensors[c]
        upwind = down * jnp.where(downward, above, below)
        sidewind = across * jnp.where(rightward, left, right)
        new.append((own[c] * here + scale * noises[c]) + (upwind + sidewind))
    xx, xy, yy = (tensor[0] for tensor in tensors)
    return (
        new[0] + (2.0 * down_across * xy + relaxed),
        new[1] + (down_across * yy + across_down * xx),
        new[2] + (2.0 * across_down * xy + relaxed),
    )


def kernel(
    fields, noise, velocity, geometry, fields_out, velocity_out,
    XN, XC, XL, XR, N, V, G, U, UE, S, PG, M_own, M_all, VR_out, VR_in, FE_out, FE_in, VC_out, VC_in,
    Q, Y_in, Z_in, T, C, C_in, E_in, K_in, local_sem, send_sem, recv_sem,
):
    f = lax.axis_index("field")
    s = lax.axis_index("space")
    zh = f // RING
    y = f % RING
    f_up, f_down = (f + 1) % TILES, (f + TILES - 1) % TILES
    s_up, s_down = (s + 1) % TILES, (s + TILES - 1) % TILES
    first, last = s == 0, s == TILES - 1

    def y_peer(d):
        return zh * RING + (y + d) % RING

    def z_peer(o):
        return (zh + o) % RING * RING + y

    def peer_back(o, d):
        return (zh + RING - o) % RING * RING + (y + RING - d) % RING

    started = []

    def send(name, source, target, to_f, to_s):
        copy = pltpu.make_async_remote_copy(
            src_ref=source,
            dst_ref=target,
            send_sem=send_sem.at[SLOTS[name]],
            recv_sem=recv_sem.at[SLOTS[name]],
            device_id=(to_f, to_s),
            device_id_type=MESH,
        )
        copy.start()
        started.append(copy)

    def arrive(name, landed):
        pltpu.make_async_copy(landed, landed, recv_sem.at[SLOTS[name]]).wait()

    barrier = pltpu.get_barrier_semaphore()
    partners = [(f, (s + d) % TILES) for d in range(1, TILES)]
    partners += [(y_peer(d), s) for d in (1, 2, 3)] + [(z_peer(d), s) for d in (1, 2, 3)]
    for partner in partners:
        pl.semaphore_signal(barrier, inc=1, device_id=partner, device_id_type=MESH)

    load_v = pltpu.make_async_copy(velocity, V, local_sem.at[0])
    load_v.start()
    load_g = pltpu.make_async_copy(geometry, G, local_sem.at[1])
    load_g.start()
    loads = []
    for c in range(3):
        loads.append(pltpu.make_async_copy(fields.at[c], XN.at[c], local_sem.at[2 + c]))
    for c in range(3):
        loads.append(pltpu.make_async_copy(noise.at[c], N.at[c], local_sem.at[5 + c]))
    for copy in loads:
        copy.start()

    lane = lax.broadcasted_iota(jnp.int32, (8, LANES), 1)
    row = lax.broadcasted_iota(jnp.int32, (8, LANES), 0)
    low = lane < TILE
    at_left, at_right = lane == 0, lane == LANES - 1
    at_top, at_bottom = row == 0, row == 7

    load_v.wait()
    own = jnp.concatenate([V[0], V[1]], axis=1)
    PG[f, 0:ROWS, :] = own
    M_own[...] = jnp.max(jnp.abs(own).reshape(ROWS // 8, 8, LANES), axis=0)
    VR_out[0, 0:8, :] = own[ROWS - 8 :]
    VR_out[1, 0:8, :] = own[0:8]

    load_g.wait()
    half = f % 2
    t_own = f // 2

    def walls(rows):
        def block(t):
            at = pl.multiple_of(jnp.clip(t, 0, COLS - 1) * LANES, LANES)
            return G[rows, pl.ds(at, LANES)].astype(F32)

        before, here, after = block(t_own - 1), block(t_own), block(t_own + 1)
        count = here.shape[0]
        at = lax.broadcasted_iota(jnp.int32, (count, LANES), 1)
        even = pltpu.roll(jnp.where(at < 120, here, before), HALO, axis=1)
        odd = pltpu.roll(jnp.where(at < HALO, after, here), HALO + TILE, axis=1)
        return jnp.where(half == 0, even, odd)

    VR_out[0, 8:16, :] = walls(slice(ROWS - 8, ROWS))
    VR_out[1, 8:16, :] = walls(slice(0, 8))

    pl.semaphore_wait(barrier, len(partners))

    send(("vrow", 0), VR_out.at[0], VR_in.at[0], f, s_up)
    send(("vrow", 1), VR_out.at[1], VR_in.at[1], f, s_down)
    for d in range(1, TILES):
        send(("max", d), M_own, M_all.at[d], f, (s + d) % TILES)
    main = PG.at[f, 0:ROWS]
    for h in range(CHUNKS):
        piece = PG.at[f, h * PIECE : (h + 1) * PIECE]
        for o in (2, 1, 3):
            send(("z", o, h), piece, piece, z_peer(o), s)
    for d in (2, 1, 3):
        send(("y", d), main, main, y_peer(d), s)

    for copy in loads:
        copy.wait()
    for t in range(COLS):
        columns = slice(t * LANES, (t + 1) * LANES)
        here = slice(t, t + 1)
        for c in range(3):
            for e in range(LOCAL):
                at = c * LOCAL + e
                for side, edge, step in ((0, ROWS - 1, -1), (1, 0, 1)):
                    second = edge + step
                    FE_out[side, at, here, :] = XN[c, e, edge : edge + 1, columns]
                    FE_out[side, 12 + at, here, :] = XN[c, e, second : second + 1, columns]
                    FE_out[side, 24 + at, here, :] = N[c, e, edge : edge + 1, columns]
        for side, edge in ((0, ROWS - 1), (1, 0)):
            FE_out[side, EDGE - 1, here, :] = G[edge : edge + 1, columns].astype(F32)
    send(("frow", 0), FE_out.at[0], FE_in.at[0], f, s_up)
    send(("frow", 1), FE_out.at[1], FE_in.at[1], f, s_down)

    for d in (0, 1):
        arrive(("vrow", d), VR_in.at[d])
    speed = M_own[...]
    for d in range(1, TILES):
        arrive(("max", d), M_all.at[d])
        speed = jnp.maximum(speed, M_all[d])
    speed = jnp.max(speed, axis=0, keepdims=True)
    above = jnp.where(first, 0.0, VR_in[0, 6:8, :])
    below = jnp.where(last, 0.0, VR_in[1, 0:2, :])
    PG[f, ROWS : ROWS + 2, :] = above
    PG[f, ROWS + 2 : ROWS + 4, :] = below
    PG[f, ROWS + 4 : PACKED, :] = jnp.broadcast_to(speed, (PACKED - ROWS - 4, LANES))
    rim = PG.at[f, ROWS:PACKED]

    def send_rim(o, d):
        send(("rim", o, d), rim, rim, (zh + o) % RING * RING + (y + d) % RING, s)

    for at in (1, 2, 3):
        send_rim(at, 0)
        send_rim(0, at)

    for h in range(CHUNKS):
        for o in (1, 3, 2):
            piece = PG.at[peer_back(o, 0), h * PIECE : (h + 1) * PIECE]
            arrive(("z", o, h), piece)
            for d in (2, 1, 3):
                send(("zy", o, d, h), piece, piece, y_peer(d), s)
            if h == 0:
                for d in (2, 1, 3):
                    send_rim(RING - o, d)
    VC_out[0:8, :] = VR_in[0, 0:8, :]
    VC_out[8:16, :] = VR_in[1, 0:8, :]
    send(("vcorner", 0), VC_out, VC_in.at[0], f_up, s)
    send(("vcorner", 1), VC_out, VC_in.at[1], f_down, s)

    def block_at(t):
        return pl.ds(pl.multiple_of(t * LANES, LANES), LANES)

    def prepare(i, carry):
        t, r = i // 8, i % 8
        rows, rows_in = pl.ds(pl.multiple_of(r * 8, 8), 8), pl.ds(pl.multiple_of(r * 8 + HALO, 8), 8)
        here_at, before_at = block_at(t), block_at(jnp.maximum(t - 1, 0))
        after_at = block_at(jnp.minimum(t + 1, COLS - 1))
        for c in range(3):
            outside = float(c != 1)
            for e in range(LOCAL):
                here = XN[c, e, rows, here_at]
                before = jnp.where(t == 0, outside, XN[c, e, rows, before_at])
                after = jnp.where(t == COLS - 1, outside, XN[c, e, rows, after_at])
                XC[c, e, t, rows_in, :] = here
                XL[c, e, t, rows, :] = pltpu.roll(jnp.where(at_right, before, here), 1, axis=1)
                XR[c, e, t, rows, :] = pltpu.roll(jnp.where(at_left, after, here), LANES - 1, axis=1)
        return carry

    lax.fori_loop(0, 64, prepare, 0)
    for t in (0, COLS + 1):
        U[:, :, t * LANES : (t + 1) * LANES] = jnp.zeros((2, TALL, LANES), F32)
        S[:, t, :, :] = jnp.zeros((3, TALL, LANES), F32)
    for d in (0, 1):
        arrive(("frow", d), FE_in.at[d])
    for c in range(3):
        outside = float(c != 1)
        for e in range(LOCAL):
            row_above = jnp.where(first, outside, FE_in[0, c * LOCAL + e])
            row_below = jnp.where(last, outside, FE_in[1, c * LOCAL + e])
            for t in range(COLS):
                XC[c, e, t, HALO - 1 : HALO, :] = row_above[t : t + 1]
                XC[c, e, t, HALO + ROWS : HALO + ROWS + 1, :] = row_below[t : t + 1]

    low_tile = lax.broadcasted_iota(jnp.int32, (PACKED, LANES), 1) < TILE
    speed = jnp.zeros((1, LANES), F32)
    for o in range(4):
        for d in range(4):
            if o or d:
                arrive(("rim", o, d), PG.at[peer_back(o, d), ROWS:PACKED])
    for o in (0, 1, 3, 2):
        for d in (1, 2, 3):
            if o == 0:
                arrive(("y", d), PG.at[peer_back(0, d), 0:ROWS])
            else:
                for h in range(CHUNKS):
                    arrive(("zy", o, d, h), PG.at[peer_back(o, d), h * PIECE : (h + 1) * PIECE])
        for tt in (0, 1):
            t = (zh + RING - o) % RING * 2 + tt
            even, odd = PG[2 * t], PG[2 * t + 1]
            u = jnp.where(low_tile, even, pltpu.roll(odd, TILE, axis=1))
            w = jnp.where(low_tile, pltpu.roll(even, TILE, axis=1), odd)
            columns = block_at(t + 1)
            for c, strip in ((0, u), (1, w)):
                U[c, HALO : HALO + ROWS, columns] = strip[0:ROWS]
                U[c, HALO - 2 : HALO, columns] = strip[ROWS : ROWS + 2]
                U[c, HALO + ROWS : HALO + ROWS + 2, columns] = strip[ROWS + 2 : ROWS + 4]
            speed = jnp.maximum(
                speed, jnp.maximum(even[ROWS + 4 : ROWS + 5], odd[ROWS + 4 : ROWS + 5])
            )
    for t in range(COLS):
        columns = slice((t + 1) * LANES, (t + 2) * LANES)
        here = slice(t, t + 1)
        for c in range(2):
            for side, rows in ((0, (HALO - 1, HALO - 2, HALO)), (1, (HALO + ROWS, HALO + ROWS - 1, HALO + ROWS + 1))):
                for q, at in enumerate(rows):
                    UE[side, c, q, here, :] = U[c, at : at + 1, columns]
    speed = jnp.max(speed, axis=1, keepdims=True)
    step = COURANT / (speed + SPEED_EPS)
    step = jnp.broadcast_to(step, (8, LANES))
    scale = jnp.sqrt(step / RELAX)

    def stress_of(total, weight):
        weight = MODULUS / FIELDS * weight
        return (
            weight * (total[0] - float(LOCAL)),
            weight * total[1],
            weight * (total[2] - float(LOCAL)),
        )

    def added(total, new):
        return new if total is None else tuple(a + b for a, b in zip(total, new))

    def spread(centre, above, below, outside):
        to_right = pltpu.roll(centre, 1, axis=1)
        to_left = pltpu.roll(centre, LANES - 1, axis=1)
        before = jnp.where(at_top, outside, pltpu.roll(to_right, 1, axis=0))
        after = jnp.where(at_bottom, outside, pltpu.roll(to_left, 7, axis=0))
        left = jnp.where(at_left, before, to_right)
        right = jnp.where(at_right, after, to_left)
        return centre, above, below, left, right

    for side, absent, place in ((0, first, HALO - 1), (1, last, HALO + ROWS)):
        weights = coefficients(step, *(spread(*(UE[side, c, q] for q in range(3)), 0.0) for c in range(2)))
        total = None
        for e in range(LOCAL):
            tensors = []
            for c in range(3):
                at = c * LOCAL + e
                centre, outer, inner = FE_in[side, at], FE_in[side, 12 + at], FE_out[1 - side, at]
                above, below = (outer, inner) if side == 0 else (inner, outer)
                tensors.append(spread(centre, above, below, float(c != 1)))
            noises = [FE_in[side, 24 + c * LOCAL + e] for c in range(3)]
            total = added(total, update(weights, scale, tensors, noises))
        for c, values in enumerate(stress_of(total, FE_in[side, EDGE - 1])):
            values = jnp.where(absent, 0.0, values)
            for t in range(COLS):
                S[c, t + 1, place : place + 1, :] = values[t : t + 1]

    def nearby(ref, lead, r, t):
        rows, columns = pl.ds(pl.multiple_of(r * 8 + HALO, 8), 8), block_at(t)
        rows_above = pl.ds(pl.multiple_of(r * 8, 8), 8)
        rows_below = pl.ds(pl.multiple_of(r * 8 + 2 * HALO, 8), 8)
        here = ref[(*lead, rows, columns)]
        above = jnp.where(at_bottom, ref[(*lead, rows_above, columns)], here)
        below = jnp.where(at_top, ref[(*lead, rows_below, columns)], here)
        left = jnp.where(at_right, ref[(*lead, rows, block_at(t - 1))], here)
        right = jnp.where(at_left, ref[(*lead, rows, block_at(t + 1))], here)
        return (
            here,
            pltpu.roll(above, 1, axis=0),
            pltpu.roll(below, 7, axis=0),
            pltpu.roll(left, 1, axis=1),
            pltpu.roll(right, LANES - 1, axis=1),
        )

    start = 2 * ((zh + 1) % RING) + COLS - 1

    def advance(i, carry):
        t = (start + i // 4) % COLS
        for part in (0, 1):
            r = i % 4 * 2 + part
            rows, columns = pl.ds(pl.multiple_of(r * 8, 8), 8), block_at(t)
            rows_in = pl.ds(pl.multiple_of(r * 8 + HALO, 8), 8)
            rows_above, rows_below = pl.ds(r * 8 + HALO - 1, 8), pl.ds(r * 8 + HALO + 1, 8)
            weights = coefficients(step, nearby(U, (0,), r, t + 1), nearby(U, (1,), r, t + 1))
            total = None
            for e in range(LOCAL):
                tensors = [
                    (
                        XC[c, e, t, rows_in, :],
                        XC[c, e, t, rows_above, :],
                        XC[c, e, t, rows_below, :],
                        XL[c, e, t, rows, :],
                        XR[c, e, t, rows, :],
                    )
                    for c in range(3)
                ]
                noises = [N[c, e, rows, columns] for c in range(3)]
                new = update(weights, scale, tensors, noises)
                for c in range(3):
                    N[c, e, rows, columns] = new[c]
                total = added(total, new)
            weight = G[rows, columns].astype(F32)
            for c, values in enumerate(stress_of(total, weight)):
                S[c, t + 1, rows_in, :] = values
        return carry

    def forces(j):
        block = (zh + 1 + j) % RING

        def body(tt, carry):
            t = 2 * block + tt + 1
            for r in range(ROWS // 8):
                top = r * 8 + HALO
                rows = slice(top, top + 8)

                def along_rows(c):
                    return S[c, t, top + 1 : top + 9, :] - S[c, t, top - 1 : top + 7, :]

                def along_cols(c):
                    here = S[c, t, rows, :]
                    left = jnp.where(at_right, S[c, t - 1, rows, :], here)
                    right = jnp.where(at_left, S[c, t + 1, rows, :], here)
                    return pltpu.roll(right, LANES - 1, axis=1) - pltpu.roll(left, 1, axis=1)

                down = 0.5 * (along_rows(0) + along_cols(1))
                across = 0.5 * (along_rows(1) + along_cols(2))
                packed = slice(r * 8, r * 8 + 8)
                Q[j, 2 * tt, packed, :] = jnp.where(low, down, pltpu.roll(across, TILE, axis=1))
                Q[j, 2 * tt + 1, packed, :] = jnp.where(low, pltpu.roll(down, TILE, axis=1), across)
            return carry

        lax.fori_loop(0, 2, body, 0)
        for d in (2, 1, 3):
            send(("part", j, d), Q.at[j, (y + d) % RING], Y_in.at[j, d - 1], y_peer(d), s)

    wide_lane = lax.broadcasted_iota(jnp.int32, (ROWS, LANES), 1)

    def edges(tile):
        turned = pltpu.roll(tile, HALO + TILE, axis=1)
        for wide in (
            jnp.where(wide_lane < 8, turned, pltpu.roll(tile, 16, axis=1)),
            jnp.where(wide_lane < 8, tile, turned),
        ):
            folded = wide[0:8]
            for block in range(1, 8):
                part = pltpu.roll(wide[8 * block : 8 * block + 8], 16 * block, axis=1)
                folded = jnp.where(lane >= 16 * block, part, folded)
            yield folded

    def ring_sum(j):
        owner = z_peer(j + 1)
        neighbours = (0, (owner + 1) % TILES), (1, (owner + TILES - 1) % TILES)
        for d in (1, 2, 3):
            arrive(("part", j, d), Y_in.at[j, d - 1])
        tile = (Q[j, y] + Y_in[j, 0]) + (Y_in[j, 1] + Y_in[j, 2])
        T[j] = tile
        ends = (0, s_up, T.at[j, ROWS - 8 : ROWS]), (1, s_down, T.at[j, 0:8])
        if j < 3:
            send(("sum", j), T.at[j], Z_in.at[j], owner, s)
        for b, to_s, rows in ends:
            for a, to_f in neighbours:
                send(("corner", a, b, j), rows, K_in.at[a, b, j], to_f, to_s)
        for b, to_s, rows in ends:
            send(("end", b, j), rows, E_in.at[b, j], owner, to_s)
        for (a, to_f), edge in zip(neighbours, edges(tile)):
            C[j, a] = edge
            send(("side", a, j), C.at[j, a], C_in.at[a, j], to_f, s)

    lax.fori_loop(0, 16, advance, 0)
    forces(0)
    lax.fori_loop(16, 24, advance, 0)
    forces(1)
    lax.fori_loop(24, 32, advance, 0)
    forces(2)
    forces(3)
    store = pltpu.make_async_copy(N, fields_out, local_sem.at[8])
    store.start()
    at_row = lax.broadcasted_iota(jnp.int32, (TALL, LANES), 0) + (s * ROWS - HALO)
    at_lane = lax.broadcasted_iota(jnp.int32, (TALL, LANES), 1)
    at_col = at_lane + (f * TILE - HALO)
    inside = (at_row >= 0) & (at_row < TILES * ROWS) & (at_col >= 0) & (at_col < TILES * TILE)
    inside = inside & (at_lane < TALL)
    for d in (0, 1):
        arrive(("vcorner", d), VC_in.at[d])

    near = lambda values: pltpu.roll(values, HALO, axis=1)
    far = lambda values: pltpu.roll(values, HALO + TILE, axis=1)

    def window(before, here, after):
        joined = jnp.where(at_lane < HALO, before, jnp.where(at_lane < HALO + TILE, here, after))
        return jnp.where(inside, joined, 0.0)

    def stacked(rim_rows, tile):
        return jnp.concatenate([rim_rows[0:8], PG[tile, 0:ROWS, :], rim_rows[8:16]], axis=0)

    v_before, v_here, v_after = (
        stacked(VC_in.at[0], f_down), stacked(VC_out, f), stacked(VC_in.at[1], f_up)
    )
    speeds = (
        window(far(v_before), near(v_here), far(v_after)),
        window(near(v_before), far(v_here), near(v_after)),
    )
    mask = jnp.concatenate([VR_in[0, 8:16, :], walls(slice(0, ROWS)), VR_in[1, 8:16, :]], axis=0)
    weight = BETA + 4.0 * VISCOSITY + PENALTY * (1.0 - mask)

    def apply(values):
        around = (
            pltpu.roll(values, TALL - 1, axis=0)
            + pltpu.roll(values, 1, axis=0)
            + pltpu.roll(values, LANES - 1, axis=1)
            + pltpu.roll(values, 1, axis=1)
        )
        return weight * values - VISCOSITY * around

    residual = [BETA * v - apply(v) for v in speeds]

    ring_sum(0)
    ring_sum(1)
    ring_sum(2)
    ring_sum(3)
    total = T[3]
    for j in range(3):
        arrive(("sum", j), Z_in.at[j])
        total = total + Z_in[j]
    for j in range(4):
        for b in (0, 1):
            for a in (0, 1):
                arrive(("corner", a, b, j), K_in.at[a, b, j])
            arrive(("end", b, j), E_in.at[b, j])
        for a in (0, 1):
            arrive(("side", a, j), C_in.at[a, j])

    def summed(ref, *lead):
        return (ref[(*lead, 0)] + ref[(*lead, 1)]) + (ref[(*lead, 2)] + ref[(*lead, 3)])

    def beside(a, turn, first, second):
        folded = summed(C_in, a)
        corners = [summed(K_in, a, b) for b in (0, 1)]
        return tuple(
            jnp.concatenate(
                [place(corners[0])]
                + [pltpu.roll(folded, (turn - 16 * block - 8 * c) % LANES, axis=1) for block in range(8)]
                + [place(corners[1])],
                axis=0,
            )
            for c, place in enumerate((first, second))
        )

    f_before = beside(0, 0, far, near)
    f_after = beside(1, HALO + TILE, far, near)
    f_here = jnp.concatenate([summed(E_in, 0), total, summed(E_in, 1)], axis=0)
    force = (
        window(f_before[0], near(f_here), f_after[0]),
        window(f_before[1], far(f_here), f_after[1]),
    )

    centre = 0.5 * (UPPER + LOWER)
    radius = 0.5 * (UPPER - LOWER)
    sigma = centre / radius
    for c in range(2):
        rho = 1.0 / sigma
        v = speeds[c]
        r = jnp.where(inside, residual[c] + force[c], 0.0)
        d = r / centre
        for index in range(ITERS):
            v = v + d
            if index + 1 < ITERS:
                r = jnp.where(inside, r - apply(d), 0.0)
                rho_next = 1.0 / (2.0 * sigma - rho)
                d = rho_next * rho * d + 2.0 * rho_next / radius * r
                rho = rho_next
        velocity_out[c, :, :] = pltpu.roll(v, LANES - HALO, axis=1)[HALO : HALO + ROWS, 0:TILE]

    for copy in started:
        copy.wait_send()
    store.wait()


def per_device(fields, increments, velocity, geometry):
    hbm = pl.BlockSpec(memory_space=pltpu.HBM)

    def vmem(*shape):
        return pltpu.VMEM(shape, F32)

    return pl.pallas_call(
        kernel,
        out_shape=(
            jax.ShapeDtypeStruct(fields.shape, F32),
            jax.ShapeDtypeStruct(velocity.shape, F32),
        ),
        in_specs=[hbm] * 4,
        out_specs=(hbm, pl.BlockSpec(memory_space=pltpu.VMEM)),
        scratch_shapes=[
            vmem(3, LOCAL, ROWS, COLS * LANES),
            vmem(3, LOCAL, COLS, TALL, LANES),
            vmem(3, LOCAL, COLS, ROWS, LANES),
            vmem(3, LOCAL, COLS, ROWS, LANES),
            vmem(3, LOCAL, ROWS, COLS * LANES),
            vmem(2, ROWS, TILE),
            pltpu.VMEM((ROWS, COLS * LANES), jnp.int32),
            vmem(2, TALL, (COLS + 2) * LANES),
            vmem(2, 2, 3, COLS, LANES),
            vmem(3, COLS + 2, TALL, LANES),
            vmem(TILES, PACKED, LANES),
            vmem(8, LANES),
            vmem(TILES, 8, LANES),
            vmem(2, 16, LANES),
            vmem(2, 16, LANES),
            vmem(2, EDGE, COLS, LANES),
            vmem(2, EDGE, COLS, LANES),
            vmem(16, LANES),
            vmem(2, 16, LANES),
            vmem(RING, RING, ROWS, LANES),
            vmem(RING, 3, ROWS, LANES),
            vmem(3, ROWS, LANES),
            vmem(RING, ROWS, LANES),
            vmem(RING, 2, 8, LANES),
            vmem(2, RING, 8, LANES),
            vmem(2, RING, 8, LANES),
            vmem(2, 2, RING, 8, LANES),
            pltpu.SemaphoreType.DMA((9,)),
            pltpu.SemaphoreType.DMA((len(SLOTS),)),
            pltpu.SemaphoreType.DMA((len(SLOTS),)),
        ],
        compiler_params=pltpu.CompilerParams(
            collective_id=0, has_side_effects=True, vmem_limit_bytes=VMEM_LIMIT
        ),
        name="step",
    )(fields, increments, velocity, geometry)


def solution(mesh):
    placed = (
        P(None, "field", "space", None),
        P(None, "field", "space", None),
        P(None, "space", "field"),
        P("space", None),
    )
    return jax.shard_map(
        per_device,
        mesh=mesh,
        in_specs=placed,
        out_specs=(P(None, "field", "space", None), P(None, "space", "field")),
        check_vma=False,
    )
```

```python
import functools

import jax
import jax.numpy as jnp
from jax import lax
from jax.experimental import pallas as pl
from jax.experimental.pallas import tpu as pltpu
from jax.sharding import PartitionSpec as P

ITERS = 8
COURANT = 0.5
SPEED_EPS = 1e-06
RELAX = 0.5
MODULUS = 2.0
BETA = 0.5
VISCOSITY = 1.0
PENALTY = 20.0
LOWER = BETA
UPPER = BETA + PENALTY + 8.0 * VISCOSITY

MESH = pl.DeviceIdType.MESH
F32 = jnp.float32
LANES = 128
ROWS = 64
HALO = 8
TALL = ROWS + 2 * HALO
TILE = 64
TILES = 16
COLS = 8
FIELDS = 64
LOCAL = 4
VMEM_LIMIT = 63 * 1024 * 1024
RING = 4
CHUNKS = 1
PIECE = ROWS // CHUNKS
PACKED = 72
EDGE = 12 * 3 + 1


def slots():
    names = [(n, d) for n in ("max",) for d in range(1, 16)]
    names += [("rim", o, d) for o in range(4) for d in range(4) if o or d]
    names += [(n, d) for n in ("vrow", "frow", "vcorner") for d in (0, 1)]
    names += [("y", d) for d in (1, 2, 3)]
    names += [("z", o, h) for o in (1, 2, 3) for h in range(CHUNKS)]
    names += [("zy", o, d, h) for o in (1, 2, 3) for d in (1, 2, 3) for h in range(CHUNKS)]
    names += [("part", j, d) for j in range(4) for d in (1, 2, 3)]
    names += [("sum", j) for j in range(3)]
    names += [(n, d, j) for n in ("side", "end") for d in (0, 1) for j in range(4)]
    names += [("corner", a, b, j) for a in (0, 1) for b in (0, 1) for j in range(4)]
    return {name: at for at, name in enumerate(names)}


SLOTS = slots()


def coefficients(step, u, w):
    (u, u_above, u_below, u_left, u_right), (w, w_above, w_below, w_left, w_right) = u, w
    half_step = 0.5 * step
    down_down = half_step * (u_below - u_above)
    down_across = half_step * (u_right - u_left)
    across_down = half_step * (w_below - w_above)
    across_across = half_step * (w_right - w_left)
    down, across = step * jnp.abs(u), step * jnp.abs(w)
    relaxed = step * (1.0 / RELAX)
    kept = 1.0 - relaxed - down - across
    own = (
        kept + 2.0 * down_down,
        kept + (down_down + across_across),
        kept + 2.0 * across_across,
    )
    return own, (u > 0.0, w > 0.0), (down, across), down_across, across_down, relaxed


def update(weights, scale, tensors, noises):
    own, (downward, rightward), (down, across), down_across, across_down, relaxed = weights
    new = []
    for c in range(3):
        here, above, below, left, right = tensors[c]
        upwind = down * jnp.where(downward, above, below)
        sidewind = across * jnp.where(rightward, left, right)
        new.append((own[c] * here + scale * noises[c]) + (upwind + sidewind))
    xx, xy, yy = (tensor[0] for tensor in tensors)
    return (
        new[0] + (2.0 * down_across * xy + relaxed),
        new[1] + (down_across * yy + across_down * xx),
        new[2] + (2.0 * across_down * xy + relaxed),
    )


def kernel(
    fields, noise, velocity, geometry, fields_out, velocity_out,
    XN, XC, XL, XR, N, V, G, U, UE, S, PG, M_own, M_all, VR_out, VR_in, FE_out, FE_in, VC_out, VC_in,
    Q, Y_in, Z_in, T, C, C_in, E_in, K_in, local_sem, send_sem, recv_sem,
):
    f = lax.axis_index("field")
    s = lax.axis_index("space")
    zh = f // RING
    y = f % RING
    f_up, f_down = (f + 1) % TILES, (f + TILES - 1) % TILES
    s_up, s_down = (s + 1) % TILES, (s + TILES - 1) % TILES
    first, last = s == 0, s == TILES - 1

    def y_peer(d):
        return zh * RING + (y + d) % RING

    def z_peer(o):
        return (zh + o) % RING * RING + y

    def peer_back(o, d):
        return (zh + RING - o) % RING * RING + (y + RING - d) % RING

    started = []

    def send(name, source, target, to_f, to_s):
        copy = pltpu.make_async_remote_copy(
            src_ref=source,
            dst_ref=target,
            send_sem=send_sem.at[SLOTS[name]],
            recv_sem=recv_sem.at[SLOTS[name]],
            device_id=(to_f, to_s),
            device_id_type=MESH,
        )
        copy.start()
        started.append(copy)

    def arrive(name, landed):
        pltpu.make_async_copy(landed, landed, recv_sem.at[SLOTS[name]]).wait()

    barrier = pltpu.get_barrier_semaphore()
    partners = [(f, (s + d) % TILES) for d in range(1, TILES)]
    partners += [(y_peer(d), s) for d in (1, 2, 3)] + [(z_peer(d), s) for d in (1, 2, 3)]
    for partner in partners:
        pl.semaphore_signal(barrier, inc=1, device_id=partner, device_id_type=MESH)

    load_v = pltpu.make_async_copy(velocity, V, local_sem.at[0])
    load_v.start()
    load_g = pltpu.make_async_copy(geometry, G, local_sem.at[1])
    load_g.start()
    loads = []
    for c in range(3):
        loads.append(pltpu.make_async_copy(fields.at[c], XN.at[c], local_sem.at[2 + c]))
    for c in range(3):
        loads.append(pltpu.make_async_copy(noise.at[c], N.at[c], local_sem.at[5 + c]))
    for copy in loads:
        copy.start()

    lane = lax.broadcasted_iota(jnp.int32, (8, LANES), 1)
    row = lax.broadcasted_iota(jnp.int32, (8, LANES), 0)
    low = lane < TILE
    at_left, at_right = lane == 0, lane == LANES - 1
    at_top, at_bottom = row == 0, row == 7

    load_v.wait()
    own = jnp.concatenate([V[0], V[1]], axis=1)
    PG[f, 0:ROWS, :] = own
    M_own[...] = jnp.max(jnp.abs(own).reshape(ROWS // 8, 8, LANES), axis=0)
    VR_out[0, 0:8, :] = own[ROWS - 8 :]
    VR_out[1, 0:8, :] = own[0:8]

    pl.semaphore_wait(barrier, len(partners))

    for d in range(1, TILES):
        send(("max", d), M_own, M_all.at[d], f, (s + d) % TILES)
    main = PG.at[f, 0:ROWS]
    for h in range(CHUNKS):
        piece = PG.at[f, h * PIECE : (h + 1) * PIECE]
        for o in (2, 1, 3):
            send(("z", o, h), piece, piece, z_peer(o), s)
    for d in (2, 1, 3):
        send(("y", d), main, main, y_peer(d), s)

    load_g.wait()
    half = f % 2
    t_own = f // 2

    def walls(rows):
        def block(t):
            at = pl.multiple_of(jnp.clip(t, 0, COLS - 1) * LANES, LANES)
            return G[rows, pl.ds(at, LANES)].astype(F32)

        before, here, after = block(t_own - 1), block(t_own), block(t_own + 1)
        count = here.shape[0]
        at = lax.broadcasted_iota(jnp.int32, (count, LANES), 1)
        even = pltpu.roll(jnp.where(at < 120, here, before), HALO, axis=1)
        odd = pltpu.roll(jnp.where(at < HALO, after, here), HALO + TILE, axis=1)
        return jnp.where(half == 0, even, odd)

    VR_out[0, 8:16, :] = walls(slice(ROWS - 8, ROWS))
    VR_out[1, 8:16, :] = walls(slice(0, 8))

    send(("vrow", 0), VR_out.at[0], VR_in.at[0], f, s_up)
    send(("vrow", 1), VR_out.at[1], VR_in.at[1], f, s_down)

    for copy in loads:
        copy.wait()
    for t in range(COLS):
        columns = slice(t * LANES, (t + 1) * LANES)
        here = slice(t, t + 1)
        for c in range(3):
            for e in range(LOCAL):
                at = c * LOCAL + e
                for side, edge, step in ((0, ROWS - 1, -1), (1, 0, 1)):
                    second = edge + step
                    FE_out[side, at, here, :] = XN[c, e, edge : edge + 1, columns]
                    FE_out[side, 12 + at, here, :] = XN[c, e, second : second + 1, columns]
                    FE_out[side, 24 + at, here, :] = N[c, e, edge : edge + 1, columns]
        for side, edge in ((0, ROWS - 1), (1, 0)):
            FE_out[side, EDGE - 1, here, :] = G[edge : edge + 1, columns].astype(F32)
    send(("frow", 0), FE_out.at[0], FE_in.at[0], f, s_up)
    send(("frow", 1), FE_out.at[1], FE_in.at[1], f, s_down)

    for d in (0, 1):
        arrive(("vrow", d), VR_in.at[d])
    speed = M_own[...]
    for d in range(1, TILES):
        arrive(("max", d), M_all.at[d])
        speed = jnp.maximum(speed, M_all[d])
    speed = jnp.max(speed, axis=0, keepdims=True)
    above = jnp.where(first, 0.0, VR_in[0, 6:8, :])
    below = jnp.where(last, 0.0, VR_in[1, 0:2, :])
    PG[f, ROWS : ROWS + 2, :] = above
    PG[f, ROWS + 2 : ROWS + 4, :] = below
    PG[f, ROWS + 4 : PACKED, :] = jnp.broadcast_to(speed, (PACKED - ROWS - 4, LANES))
    rim = PG.at[f, ROWS:PACKED]

    def send_rim(o, d):
        send(("rim", o, d), rim, rim, (zh + o) % RING * RING + (y + d) % RING, s)

    for at in (1, 2, 3):
        send_rim(at, 0)
        send_rim(0, at)

    for h in range(CHUNKS):
        for o in (1, 3, 2):
            piece = PG.at[peer_back(o, 0), h * PIECE : (h + 1) * PIECE]
            arrive(("z", o, h), piece)
            for d in (2, 1, 3):
                send(("zy", o, d, h), piece, piece, y_peer(d), s)
            if h == 0:
                for d in (2, 1, 3):
                    send_rim(RING - o, d)
    VC_out[0:8, :] = VR_in[0, 0:8, :]
    VC_out[8:16, :] = VR_in[1, 0:8, :]
    send(("vcorner", 0), VC_out, VC_in.at[0], f_up, s)
    send(("vcorner", 1), VC_out, VC_in.at[1], f_down, s)

    def block_at(t):
        return pl.ds(pl.multiple_of(t * LANES, LANES), LANES)

    def prepare(i, carry):
        t, r = i // 8, i % 8
        rows, rows_in = pl.ds(pl.multiple_of(r * 8, 8), 8), pl.ds(pl.multiple_of(r * 8 + HALO, 8), 8)
        here_at, before_at = block_at(t), block_at(jnp.maximum(t - 1, 0))
        after_at = block_at(jnp.minimum(t + 1, COLS - 1))
        for c in range(3):
            outside = float(c != 1)
            for e in range(LOCAL):
                here = XN[c, e, rows, here_at]
                before = jnp.where(t == 0, outside, XN[c, e, rows, before_at])
                after = jnp.where(t == COLS - 1, outside, XN[c, e, rows, after_at])
                XC[c, e, t, rows_in, :] = here
                XL[c, e, t, rows, :] = pltpu.roll(jnp.where(at_right, before, here), 1, axis=1)
                XR[c, e, t, rows, :] = pltpu.roll(jnp.where(at_left, after, here), LANES - 1, axis=1)
        return carry

    lax.fori_loop(0, 64, prepare, 0)
    for t in (0, COLS + 1):
        U[:, :, t * LANES : (t + 1) * LANES] = jnp.zeros((2, TALL, LANES), F32)
        S[:, t, :, :] = jnp.zeros((3, TALL, LANES), F32)
    for d in (0, 1):
        arrive(("frow", d), FE_in.at[d])
    for c in range(3):
        outside = float(c != 1)
        for e in range(LOCAL):
            row_above = jnp.where(first, outside, FE_in[0, c * LOCAL + e])
            row_below = jnp.where(last, outside, FE_in[1, c * LOCAL + e])
            for t in range(COLS):
                XC[c, e, t, HALO - 1 : HALO, :] = row_above[t : t + 1]
                XC[c, e, t, HALO + ROWS : HALO + ROWS + 1, :] = row_below[t : t + 1]

    low_tile = lax.broadcasted_iota(jnp.int32, (PACKED, LANES), 1) < TILE
    speed = jnp.zeros((1, LANES), F32)
    for o in range(4):
        for d in range(4):
            if o or d:
                arrive(("rim", o, d), PG.at[peer_back(o, d), ROWS:PACKED])
    for o in (0, 1, 3, 2):
        for d in (1, 2, 3):
            if o == 0:
                arrive(("y", d), PG.at[peer_back(0, d), 0:ROWS])
            else:
                for h in range(CHUNKS):
                    arrive(("zy", o, d, h), PG.at[peer_back(o, d), h * PIECE : (h + 1) * PIECE])
        for tt in (0, 1):
            t = (zh + RING - o) % RING * 2 + tt
            even, odd = PG[2 * t], PG[2 * t + 1]
            u = jnp.where(low_tile, even, pltpu.roll(odd, TILE, axis=1))
            w = jnp.where(low_tile, pltpu.roll(even, TILE, axis=1), odd)
            columns = block_at(t + 1)
            for c, strip in ((0, u), (1, w)):
                U[c, HALO : HALO + ROWS, columns] = strip[0:ROWS]
                U[c, HALO - 2 : HALO, columns] = strip[ROWS : ROWS + 2]
                U[c, HALO + ROWS : HALO + ROWS + 2, columns] = strip[ROWS + 2 : ROWS + 4]
            speed = jnp.maximum(
                speed, jnp.maximum(even[ROWS + 4 : ROWS + 5], odd[ROWS + 4 : ROWS + 5])
            )
    for t in range(COLS):
        columns = slice((t + 1) * LANES, (t + 2) * LANES)
        here = slice(t, t + 1)
        for c in range(2):
            for side, rows in ((0, (HALO - 1, HALO - 2, HALO)), (1, (HALO + ROWS, HALO + ROWS - 1, HALO + ROWS + 1))):
                for q, at in enumerate(rows):
                    UE[side, c, q, here, :] = U[c, at : at + 1, columns]
    speed = jnp.max(speed, axis=1, keepdims=True)
    step = COURANT / (speed + SPEED_EPS)
    step = jnp.broadcast_to(step, (8, LANES))
    scale = jnp.sqrt(step / RELAX)

    def stress_of(total, weight):
        weight = MODULUS / FIELDS * weight
        return (
            weight * (total[0] - float(LOCAL)),
            weight * total[1],
            weight * (total[2] - float(LOCAL)),
        )

    def added(total, new):
        return new if total is None else tuple(a + b for a, b in zip(total, new))

    def spread(centre, above, below, outside):
        to_right = pltpu.roll(centre, 1, axis=1)
        to_left = pltpu.roll(centre, LANES - 1, axis=1)
        before = jnp.where(at_top, outside, pltpu.roll(to_right, 1, axis=0))
        after = jnp.where(at_bottom, outside, pltpu.roll(to_left, 7, axis=0))
        left = jnp.where(at_left, before, to_right)
        right = jnp.where(at_right, after, to_left)
        return centre, above, below, left, right

    for side, absent, place in ((0, first, HALO - 1), (1, last, HALO + ROWS)):
        weights = coefficients(step, *(spread(*(UE[side, c, q] for q in range(3)), 0.0) for c in range(2)))
        total = None
        for e in range(LOCAL):
            tensors = []
            for c in range(3):
                at = c * LOCAL + e
                centre, outer, inner = FE_in[side, at], FE_in[side, 12 + at], FE_out[1 - side, at]
                above, below = (outer, inner) if side == 0 else (inner, outer)
                tensors.append(spread(centre, above, below, float(c != 1)))
            noises = [FE_in[side, 24 + c * LOCAL + e] for c in range(3)]
            total = added(total, update(weights, scale, tensors, noises))
        for c, values in enumerate(stress_of(total, FE_in[side, EDGE - 1])):
            values = jnp.where(absent, 0.0, values)
            for t in range(COLS):
                S[c, t + 1, place : place + 1, :] = values[t : t + 1]

    def nearby(ref, lead, r, t):
        rows, columns = pl.ds(pl.multiple_of(r * 8 + HALO, 8), 8), block_at(t)
        rows_above = pl.ds(pl.multiple_of(r * 8, 8), 8)
        rows_below = pl.ds(pl.multiple_of(r * 8 + 2 * HALO, 8), 8)
        here = ref[(*lead, rows, columns)]
        above = jnp.where(at_bottom, ref[(*lead, rows_above, columns)], here)
        below = jnp.where(at_top, ref[(*lead, rows_below, columns)], here)
        left = jnp.where(at_right, ref[(*lead, rows, block_at(t - 1))], here)
        right = jnp.where(at_left, ref[(*lead, rows, block_at(t + 1))], here)
        return (
            here,
            pltpu.roll(above, 1, axis=0),
            pltpu.roll(below, 7, axis=0),
            pltpu.roll(left, 1, axis=1),
            pltpu.roll(right, LANES - 1, axis=1),
        )

    start = 2 * ((zh + 1) % RING) + COLS - 1

    def advance(i, carry):
        t = (start + i // 4) % COLS
        for part in (0, 1):
            r = i % 4 * 2 + part
            rows, columns = pl.ds(pl.multiple_of(r * 8, 8), 8), block_at(t)
            rows_in = pl.ds(pl.multiple_of(r * 8 + HALO, 8), 8)
            rows_above, rows_below = pl.ds(r * 8 + HALO - 1, 8), pl.ds(r * 8 + HALO + 1, 8)
            weights = coefficients(step, nearby(U, (0,), r, t + 1), nearby(U, (1,), r, t + 1))
            total = None
            for e in range(LOCAL):
                tensors = [
                    (
                        XC[c, e, t, rows_in, :],
                        XC[c, e, t, rows_above, :],
                        XC[c, e, t, rows_below, :],
                        XL[c, e, t, rows, :],
                        XR[c, e, t, rows, :],
                    )
                    for c in range(3)
                ]
                noises = [N[c, e, rows, columns] for c in range(3)]
                new = update(weights, scale, tensors, noises)
                for c in range(3):
                    N[c, e, rows, columns] = new[c]
                total = added(total, new)
            weight = G[rows, columns].astype(F32)
            for c, values in enumerate(stress_of(total, weight)):
                S[c, t + 1, rows_in, :] = values
        return carry

    def forces(j):
        block = (zh + 1 + j) % RING

        def body(tt, carry):
            t = 2 * block + tt + 1
            for r in range(ROWS // 8):
                top = r * 8 + HALO
                rows = slice(top, top + 8)

                def along_rows(c):
                    return S[c, t, top + 1 : top + 9, :] - S[c, t, top - 1 : top + 7, :]

                def along_cols(c):
                    here = S[c, t, rows, :]
                    left = jnp.where(at_right, S[c, t - 1, rows, :], here)
                    right = jnp.where(at_left, S[c, t + 1, rows, :], here)
                    return pltpu.roll(right, LANES - 1, axis=1) - pltpu.roll(left, 1, axis=1)

                down = 0.5 * (along_rows(0) + along_cols(1))
                across = 0.5 * (along_rows(1) + along_cols(2))
                packed = slice(r * 8, r * 8 + 8)
                Q[j, 2 * tt, packed, :] = jnp.where(low, down, pltpu.roll(across, TILE, axis=1))
                Q[j, 2 * tt + 1, packed, :] = jnp.where(low, pltpu.roll(down, TILE, axis=1), across)
            return carry

        lax.fori_loop(0, 2, body, 0)
        for d in (2, 1, 3):
            send(("part", j, d), Q.at[j, (y + d) % RING], Y_in.at[j, d - 1], y_peer(d), s)

    wide_lane = lax.broadcasted_iota(jnp.int32, (ROWS, LANES), 1)

    def edges(tile):
        turned = pltpu.roll(tile, HALO + TILE, axis=1)
        for wide in (
            jnp.where(wide_lane < 8, turned, pltpu.roll(tile, 16, axis=1)),
            jnp.where(wide_lane < 8, tile, turned),
        ):
            folded = wide[0:8]
            for block in range(1, 8):
                part = pltpu.roll(wide[8 * block : 8 * block + 8], 16 * block, axis=1)
                folded = jnp.where(lane >= 16 * block, part, folded)
            yield folded

    def ring_sum(j):
        owner = z_peer(j + 1)
        neighbours = (0, (owner + 1) % TILES), (1, (owner + TILES - 1) % TILES)
        for d in (1, 2, 3):
            arrive(("part", j, d), Y_in.at[j, d - 1])
        tile = (Q[j, y] + Y_in[j, 0]) + (Y_in[j, 1] + Y_in[j, 2])
        T[j] = tile
        ends = (0, s_up, T.at[j, ROWS - 8 : ROWS]), (1, s_down, T.at[j, 0:8])
        if j < 3:
            send(("sum", j), T.at[j], Z_in.at[j], owner, s)
        for b, to_s, rows in ends:
            for a, to_f in neighbours:
                send(("corner", a, b, j), rows, K_in.at[a, b, j], to_f, to_s)
        for b, to_s, rows in ends:
            send(("end", b, j), rows, E_in.at[b, j], owner, to_s)
        for (a, to_f), edge in zip(neighbours, edges(tile)):
            C[j, a] = edge
            send(("side", a, j), C.at[j, a], C_in.at[a, j], to_f, s)

    lax.fori_loop(0, 16, advance, 0)
    forces(0)
    lax.fori_loop(16, 24, advance, 0)
    forces(1)
    lax.fori_loop(24, 32, advance, 0)
    forces(2)
    forces(3)
    store = pltpu.make_async_copy(N, fields_out, local_sem.at[8])
    store.start()
    at_row = lax.broadcasted_iota(jnp.int32, (TALL, LANES), 0) + (s * ROWS - HALO)
    at_lane = lax.broadcasted_iota(jnp.int32, (TALL, LANES), 1)
    at_col = at_lane + (f * TILE - HALO)
    inside = (at_row >= 0) & (at_row < TILES * ROWS) & (at_col >= 0) & (at_col < TILES * TILE)
    inside = inside & (at_lane < TALL)
    for d in (0, 1):
        arrive(("vcorner", d), VC_in.at[d])

    near = lambda values: pltpu.roll(values, HALO, axis=1)
    far = lambda values: pltpu.roll(values, HALO + TILE, axis=1)

    def window(before, here, after):
        joined = jnp.where(at_lane < HALO, before, jnp.where(at_lane < HALO + TILE, here, after))
        return jnp.where(inside, joined, 0.0)

    def stacked(rim_rows, tile):
        return jnp.concatenate([rim_rows[0:8], PG[tile, 0:ROWS, :], rim_rows[8:16]], axis=0)

    v_before, v_here, v_after = (
        stacked(VC_in.at[0], f_down), stacked(VC_out, f), stacked(VC_in.at[1], f_up)
    )
    speeds = (
        window(far(v_before), near(v_here), far(v_after)),
        window(near(v_before), far(v_here), near(v_after)),
    )
    mask = jnp.concatenate([VR_in[0, 8:16, :], walls(slice(0, ROWS)), VR_in[1, 8:16, :]], axis=0)
    weight = BETA + 4.0 * VISCOSITY + PENALTY * (1.0 - mask)

    def apply(values):
        around = (
            pltpu.roll(values, TALL - 1, axis=0)
            + pltpu.roll(values, 1, axis=0)
            + pltpu.roll(values, LANES - 1, axis=1)
            + pltpu.roll(values, 1, axis=1)
        )
        return weight * values - VISCOSITY * around

    residual = [BETA * v - apply(v) for v in speeds]

    ring_sum(0)
    ring_sum(1)
    ring_sum(2)
    ring_sum(3)
    total = T[3]
    for j in range(3):
        arrive(("sum", j), Z_in.at[j])
        total = total + Z_in[j]
    for j in range(4):
        for b in (0, 1):
            for a in (0, 1):
                arrive(("corner", a, b, j), K_in.at[a, b, j])
            arrive(("end", b, j), E_in.at[b, j])
        for a in (0, 1):
            arrive(("side", a, j), C_in.at[a, j])

    def summed(ref, *lead):
        return (ref[(*lead, 0)] + ref[(*lead, 1)]) + (ref[(*lead, 2)] + ref[(*lead, 3)])

    def beside(a, turn, first, second):
        folded = summed(C_in, a)
        corners = [summed(K_in, a, b) for b in (0, 1)]
        return tuple(
            jnp.concatenate(
                [place(corners[0])]
                + [pltpu.roll(folded, (turn - 16 * block - 8 * c) % LANES, axis=1) for block in range(8)]
                + [place(corners[1])],
                axis=0,
            )
            for c, place in enumerate((first, second))
        )

    f_before = beside(0, 0, far, near)
    f_after = beside(1, HALO + TILE, far, near)
    f_here = jnp.concatenate([summed(E_in, 0), total, summed(E_in, 1)], axis=0)
    force = (
        window(f_before[0], near(f_here), f_after[0]),
        window(f_before[1], far(f_here), f_after[1]),
    )

    centre = 0.5 * (UPPER + LOWER)
    radius = 0.5 * (UPPER - LOWER)
    sigma = centre / radius
    for c in range(2):
        rho = 1.0 / sigma
        v = speeds[c]
        r = jnp.where(inside, residual[c] + force[c], 0.0)
        d = r / centre
        for index in range(ITERS):
            v = v + d
            if index + 1 < ITERS:
                r = jnp.where(inside, r - apply(d), 0.0)
                rho_next = 1.0 / (2.0 * sigma - rho)
                d = rho_next * rho * d + 2.0 * rho_next / radius * r
                rho = rho_next
        velocity_out[c, :, :] = pltpu.roll(v, LANES - HALO, axis=1)[HALO : HALO + ROWS, 0:TILE]

    for copy in started:
        copy.wait_send()
    store.wait()


def per_device(fields, increments, velocity, geometry):
    hbm = pl.BlockSpec(memory_space=pltpu.HBM)

    def vmem(*shape):
        return pltpu.VMEM(shape, F32)

    return pl.pallas_call(
        kernel,
        out_shape=(
            jax.ShapeDtypeStruct(fields.shape, F32),
            jax.ShapeDtypeStruct(velocity.shape, F32),
        ),
        in_specs=[hbm] * 4,
        out_specs=(hbm, pl.BlockSpec(memory_space=pltpu.VMEM)),
        scratch_shapes=[
            vmem(3, LOCAL, ROWS, COLS * LANES),
            vmem(3, LOCAL, COLS, TALL, LANES),
            vmem(3, LOCAL, COLS, ROWS, LANES),
            vmem(3, LOCAL, COLS, ROWS, LANES),
            vmem(3, LOCAL, ROWS, COLS * LANES),
            vmem(2, ROWS, TILE),
            pltpu.VMEM((ROWS, COLS * LANES), jnp.int32),
            vmem(2, TALL, (COLS + 2) * LANES),
            vmem(2, 2, 3, COLS, LANES),
            vmem(3, COLS + 2, TALL, LANES),
            vmem(TILES, PACKED, LANES),
            vmem(8, LANES),
            vmem(TILES, 8, LANES),
            vmem(2, 16, LANES),
            vmem(2, 16, LANES),
            vmem(2, EDGE, COLS, LANES),
            vmem(2, EDGE, COLS, LANES),
            vmem(16, LANES),
            vmem(2, 16, LANES),
            vmem(RING, RING, ROWS, LANES),
            vmem(RING, 3, ROWS, LANES),
            vmem(3, ROWS, LANES),
            vmem(RING, ROWS, LANES),
            vmem(RING, 2, 8, LANES),
            vmem(2, RING, 8, LANES),
            vmem(2, RING, 8, LANES),
            vmem(2, 2, RING, 8, LANES),
            pltpu.SemaphoreType.DMA((9,)),
            pltpu.SemaphoreType.DMA((len(SLOTS),)),
            pltpu.SemaphoreType.DMA((len(SLOTS),)),
        ],
        compiler_params=pltpu.CompilerParams(
            collective_id=0, has_side_effects=True, vmem_limit_bytes=VMEM_LIMIT
        ),
        name="step",
    )(fields, increments, velocity, geometry)


def solution(mesh):
    placed = (
        P(None, "field", "space", None),
        P(None, "field", "space", None),
        P(None, "space", "field"),
        P("space", None),
    )
    return jax.shard_map(
        per_device,
        mesh=mesh,
        in_specs=placed,
        out_specs=(P(None, "field", "space", None), P(None, "space", "field")),
        check_vma=False,
    )
```
